256 devices in a mesh: chan: 16 (over x, z_hi), band: 16 (over z_lo, y, core).
Axes of the slice: x: 4, y: 4, z: 8 (z_hi: 4, z_lo: 2; z = z_hi * 2 + z_lo), core: 2. Of those that a mesh axis runs over, the one named last changes fastest.
Arguments:
- spectra: bfloat16 [32, 2, 8192, 512], P('band', None, 'chan'), may hold values from -64 to 64
- half_width: int32 [512], replicated, may hold values from 1 to 32, as said below
- panel_block: int32 [4], replicated, may hold values from 0 to 15
- panel_offset: int32 [4], replicated, may hold values from 0 to 256
Outputs:
- cross: bfloat16 [4, 32, 2, 8192, 256], P(None, 'band', None, 'chan')
The draws below stay inside these ranges and needn't reach their ends.
Inputs may be any that keep to these rules, and one draw needn't show every extreme that they name: `half_width`: some window's half-width is exactly 32.
All inputs are finite; a program needn't handle non-finite values.
Results may differ from the reference program's by a relative error of at most 0.0056.
Values may be sent and summed in bfloat16 or wider, within the bound.
A program may use at most 64 MiB of HBM per device.

```python
import math
import jax
import jax.numpy as jnp
import numpy as np
from jax import lax

CH_DEV = 512
W = 512
PANEL = 256
NPANEL = 4
HALO = 32
CHANNELS = 8192
NF = 32
N_CHAN = 16


def draw_spectra(key, part):
    keys = jax.random.split(jax.random.fold_in(key, 11), 4)
    position = jnp.arange(NF, dtype=jnp.float32) / max(NF - 1, 1)
    bin_amp = 3.0 ** position * jnp.exp(jax.random.uniform(keys[0], (NF,), jnp.float32, jnp.log(0.7), jnp.log(1.4)))
    chan_amp = jnp.exp(jax.random.uniform(keys[1], (CHANNELS,), jnp.float32, jnp.log(0.5), jnp.log(2.0)))
    win_amp = jnp.exp(jax.random.uniform(keys[2], (W,), jnp.float32, jnp.log(0.5), jnp.log(2.0)))
    noise = jnp.clip(jax.random.normal(keys[3], (NF, 2, CHANNELS, W), jnp.float32), -4.0, 4.0)
    values = noise * bin_amp[:, None, None, None] * chan_amp[None, None, :, None] * win_amp[None, None, None, :]
    return jnp.clip(values, -64.0, 64.0).astype(jnp.bfloat16)


def draw_half_width(key, part):
    keys = jax.random.split(jax.random.fold_in(key, 23), 2)
    widths = jax.random.randint(keys[0], (W,), 1, HALO + 1, dtype=jnp.int32)
    where_top = jax.random.randint(keys[1], (), 0, W, dtype=jnp.int32)
    return widths.at[where_top].set(HALO)


def touch_ends(drawn, rng, low, high):
    spot = [jax.random.randint(jax.random.fold_in(rng, axis), (), 0, length) for axis, length in enumerate(drawn.shape)]
    widest = drawn.shape.index(max(drawn.shape))
    neighbour = spot[:widest] + [(spot[widest] + 1) % drawn.shape[widest]] + spot[widest + 1:]
    return drawn.at[tuple(spot)].set(low).at[tuple(neighbour)].set(high)


def rank_table(count, slope):
    loads = [(1 << 20) // math.isqrt(rank ** slope) + 1 for rank in range(1, count + 1)]
    deviation = 1 + sum(loads) // (1 << 30)
    return np.cumsum(np.array([max(1, weight // deviation) for weight in loads]))


def skewed_ids(key, shape, count, lean):
    grid = rank_table(count, lean)
    pick = jax.random.randint(jax.random.fold_in(key, 1), shape, 0, int(grid[count - 1]))
    grade = jnp.searchsorted(jnp.asarray(grid, jnp.int32), pick, side="right")
    return jax.random.permutation(jax.random.fold_in(key, 2), count)[grade].astype(jnp.int32)


def setup_inputs(seed: int = 0) -> dict:
    seeds = jax.random.split(jax.random.key(seed), 5)
    return {
        "spectra": draw_spectra(jax.random.fold_in(seeds[4], 71), 0),
        "half_width": draw_half_width(jax.random.fold_in(seeds[4], 71), 0),
        "panel_block": touch_ends(skewed_ids(seeds[2], (NPANEL,), N_CHAN, 2), jax.random.fold_in(seeds[2], 3), 0, N_CHAN - 1).astype(jnp.int32),
        "panel_offset": touch_ends(jax.random.randint(seeds[3], (NPANEL,), 0, CH_DEV - PANEL + 1), jax.random.fold_in(seeds[3], 1), 0, CH_DEV - PANEL).astype(jnp.int32),
    }


def norm_scale(power, widths):
    padded = jnp.pad(power, ((HALO, HALO), (0, 0)))
    total = jnp.zeros_like(power)
    for offset in range(-HALO, HALO + 1):
        window = padded[HALO + offset:HALO + offset + CHANNELS]
        total = total + jnp.where(abs(offset) <= widths[None, :], window, jnp.float32(0.0))
    chan_index = jnp.arange(CHANNELS, dtype=jnp.int32)[:, None]
    count = jnp.minimum(chan_index + widths[None, :], CHANNELS - 1) - jnp.maximum(chan_index - widths[None, :], 0) + 1
    return lax.rsqrt(total / (count.astype(jnp.float32) * NF) + 1e-06)

def cross_bin(pair):
    normed_bin, source_bin = pair
    left = normed_bin.reshape(2 * CHANNELS, W).astype(jnp.float32)
    right = source_bin.reshape(2 * PANEL, W).astype(jnp.float32)
    grams = jnp.dot(left, right.T)
    real_part = grams[:CHANNELS, :PANEL] + grams[CHANNELS:, PANEL:]
    imag_part = grams[CHANNELS:, :PANEL] - grams[:CHANNELS, PANEL:]
    return (jnp.stack([real_part, imag_part]) * W ** (-0.5)).astype(jnp.bfloat16)

def reference(spectra, half_width, panel_block, panel_offset):
    values = spectra.astype(jnp.float32)
    power = lax.optimization_barrier(jnp.sum(values * values, axis=(0, 1)))
    scale = norm_scale(power, half_width)
    normed = (values * scale[None, None]).astype(jnp.bfloat16)
    results = []
    for panel in range(NPANEL):
        start = (panel_block[panel] * CH_DEV + panel_offset[panel]).astype(jnp.int32)
        source = lax.dynamic_slice_in_dim(normed, start, PANEL, 2)
        results.append(lax.map(cross_bin, (normed, source)))
    return jnp.stack(results)
```

```python
import jax
import jax.numpy as jnp
from jax import lax
from jax.experimental import pallas as pl
from jax.experimental.pallas import tpu as pltpu
from jax.sharding import PartitionSpec as P

MESH = pl.DeviceIdType.MESH
PANEL = 256
NPANEL = 4
HALO = 32
ROWS = 512
WIN = 512
Q = 128
NX = 4
NZ = 4
NCHAN = 16
NBAND = 16
PLANES = 4
CHANNELS = ROWS * NCHAN
BINS = 32
F32 = jnp.float32
BF16 = jnp.bfloat16


def move_kernel(
    spec, width, block, offset, gath, means,
    a0, a1, a2, a3, b0, b1, b2, b3, picked, onehot, power, bands, total, ms, parts, sel, wide,
    a_s, a_r, rz_s, rz_r, gz_s, gz_r, gx_s, gx_r, e_s, e_r, rb_s, rb_r, rc_s, rc_r, gc_s, gc_r, gb_s, gb_r,
):
    c, b = lax.axis_index("chan"), lax.axis_index("band")
    x, z = c // NZ, c % NZ
    rq, wq = b // 4, b % 4
    a, zb = (a0, a1, a2, a3), (b0, b1, b2, b3)

    def at_x(d):
        return ((x + d) % NX * NZ + z, b)

    def at_z(d):
        return (x * NZ + (z + d) % NZ, b)

    def at_c(d):
        return ((c + d) % NCHAN, b)

    def at_b(d):
        return (c, (b + d) % NBAND)

    def send(src, dst, ssem, rsem, dev):
        copy = pltpu.make_async_remote_copy(
            src_ref=src, dst_ref=dst, send_sem=ssem, recv_sem=rsem, device_id=dev, device_id_type=MESH
        )
        copy.start()
        return copy

    barrier = pltpu.get_barrier_semaphore()
    for d in range(1, NCHAN):
        pl.semaphore_signal(barrier, inc=1, device_id=at_c(d), device_id_type=MESH)
    for d in range(1, NBAND):
        pl.semaphore_signal(barrier, inc=1, device_id=at_b(d), device_id_type=MESH)

    def local_power(lo, count):
        acc = jnp.zeros((count, WIN), F32)
        for f in range(2):
            for k in range(2):
                v = spec[f, k, pl.ds(lo, count), :].astype(F32)
                acc = acc + v * v
        power[pl.ds(lo + HALO, count), :] = acc.astype(BF16)

    local_power(0, HALO)
    local_power(ROWS - HALO, HALO)
    pl.semaphore_wait(barrier, NCHAN + NBAND - 2)

    pending = []

    a_cp = []
    for q in range(PLANES):
        f, k = q // 2, q % 2
        row = []
        for d in (1, 3, 2):
            cols = pl.ds(pl.multiple_of((x + d) % NX * Q, Q), Q)
            row.append(send(spec.at[f, k, :, cols], a[q].at[d], a_s.at[q, d], a_r.at[q, d], at_x(d)))
        a_cp.append(row)
    up = send(power.at[pl.ds(ROWS, HALO)], power.at[pl.ds(0, HALO)], e_s.at[0], e_r.at[0], at_c(1))
    down = send(
        power.at[pl.ds(HALO, HALO)], power.at[pl.ds(ROWS + HALO, HALO)], e_s.at[1], e_r.at[1], at_c(NCHAN - 1)
    )

    def body(i, carry):
        local_power(pl.multiple_of(i * HALO, HALO), HALO)
        return carry

    lax.fori_loop(1, ROWS // HALO - 1, body, 0)
    own_cols = pl.ds(pl.multiple_of(x * Q, Q), Q)
    for q in range(PLANES):
        a[q][0] = spec[q // 2, q % 2, :, own_cols]
    for p in range(NPANEL):
        here = lax.broadcasted_iota(jnp.int32, (PANEL, ROWS), 1)
        want = lax.broadcasted_iota(jnp.int32, (PANEL, ROWS), 0) + offset[p]
        onehot[p] = jnp.where(here == want, 1.0, 0.0).astype(BF16)

    up.wait_recv()
    down.wait_recv()
    rb = []
    for d in range(1, NBAND):
        t = (b + d) % NBAND
        src = power.at[pl.ds(pl.multiple_of(t // 4 * Q, Q), Q + 2 * HALO), pl.ds(pl.multiple_of(t % 4 * Q, Q), Q)]
        rb.append(send(src, bands.at[d], rb_s.at[d], rb_r.at[d], at_b(d)))
    pending += [up, down]

    def pick(q):
        for cp in a_cp[q]:
            cp.wait_recv()
        for p in range(NPANEL):
            slot = lax.rem(x - block[p] // NZ + NX, NX)
            picked[q, p] = jnp.dot(onehot[p], a[q][slot], preferred_element_type=F32).astype(BF16)
        zb[q][0] = picked[q, :, pl.ds(pl.multiple_of(z * 64, 64), 64), :]
        out = []
        for d in (1, 3, 2):
            rows = pl.ds(pl.multiple_of((z + d) % NZ * 64, 64), 64)
            out.append(send(picked.at[q, :, rows, :], zb[q].at[d], rz_s.at[q, d], rz_r.at[q, d], at_z(d)))
        return out

    own_rows = pl.ds(pl.multiple_of(z * 64, 64), 64)

    def share_z(q, copies):
        f, k = q // 2, q % 2
        for cp in copies:
            cp.wait_recv()
        for p in range(NPANEL):
            slot = lax.rem(z - block[p] % NZ + NZ, NZ)
            gath[f, p, k, own_rows, own_cols] = zb[q][slot, p]
        out = []
        for d in (1, 3, 2):
            part = gath.at[f, :, k, own_rows, own_cols]
            out.append(send(part, part, gz_s.at[q, d], gz_r.at[q, d], at_z(d)))
        return out

    def share_x(q, copies):
        f, k = q // 2, q % 2
        for cp in copies:
            cp.wait_recv()
        part = gath.at[f, :, k, :, own_cols]
        right = send(part, part, gx_s.at[q, 0], gx_r.at[q, 0], at_x(1))
        left = send(part, part, gx_s.at[q, 1], gx_r.at[q, 1], at_x(3))
        return [right, left]

    def pass_x(q, copies):
        f, k = q // 2, q % 2
        right, left = copies
        right.wait_recv()
        cols = pl.ds(pl.multiple_of((x + 3) % NX * Q, Q), Q)
        part = gath.at[f, pl.ds(0, 2), k, :, cols]
        on_right = send(part, part, gx_s.at[q, 2], gx_r.at[q, 2], at_x(1))
        left.wait_recv()
        cols = pl.ds(pl.multiple_of((x + 1) % NX * Q, Q), Q)
        part = gath.at[f, pl.ds(2, 2), k, :, cols]
        on_left = send(part, part, gx_s.at[q, 3], gx_r.at[q, 3], at_x(3))
        return [on_right, on_left]

    rz, gz, gx, fx = [None] * 4, [None] * 4, [None] * 4, [None] * 4
    rz[0] = pick(0)

    for cp in rb:
        cp.wait_recv()
    acc = power[
        pl.ds(pl.multiple_of(rq * Q, Q), Q + 2 * HALO), pl.ds(pl.multiple_of(wq * Q, Q), Q)
    ].astype(F32)
    for d in range(1, NBAND):
        acc = acc + bands[d].astype(F32)
    first = c * ROWS + rq * Q
    chan = lax.broadcasted_iota(jnp.int32, (Q + 2 * HALO, Q), 0) + (first - HALO)
    total[...] = jnp.where((chan >= 0) & (chan < CHANNELS), acc, 0.0)
    half = width[:, pl.ds(pl.multiple_of(wq * Q, Q), Q)]
    win = total[HALO : HALO + Q, :]
    for o in range(1, HALO + 1):
        both = total[HALO - o : HALO - o + Q, :] + total[HALO + o : HALO + o + Q, :]
        win = win + jnp.where(half >= o, both, 0.0)
    chan = lax.broadcasted_iota(jnp.int32, (Q, Q), 0) + first
    count = jnp.minimum(chan + half, CHANNELS - 1) - jnp.maximum(chan - half, 0) + 1
    mean = win / (count.astype(F32) * BINS) + 1e-6
    ms[...] = mean
    my_rows = pl.ds(pl.multiple_of(rq * Q, Q), Q)
    my_cols = pl.ds(pl.multiple_of(wq * Q, Q), Q)
    means[0, my_rows, my_cols] = mean.astype(BF16)
    rc = []
    for d in range(1, NCHAN):
        src = ms.at[pl.ds(pl.multiple_of((c + d) % NCHAN * 8, 8), 8)]
        rc.append(send(src, parts.at[d], rc_s.at[d], rc_r.at[d], at_c(d)))
    parts[0] = ms[pl.ds(pl.multiple_of(c * 8, 8), 8), :]

    rz[1] = pick(1)
    gz[0] = share_z(0, rz[0])

    for cp in rc:
        cp.wait_recv()
    sel[...] = jnp.concatenate([parts[lax.rem(c - block[p] + NCHAN, NCHAN)] for p in range(NPANEL)], axis=0).astype(BF16)
    gc = []
    for d in range(1, NCHAN):
        gc.append(send(sel, wide.at[c], gc_s.at[d], gc_r.at[d], at_c(d)))
    wide[c] = sel[...]

    rz[2] = pick(2)
    gz[1] = share_z(1, rz[1])
    gx[0] = share_x(0, gz[0])

    for cp in gc:
        cp.wait_recv()
    every = wide[...].astype(F32)
    for p in range(NPANEL):
        means[1 + p, my_rows, my_cols] = every[:, p * 8 : p * 8 + 8, :].reshape(Q, Q).astype(BF16)
    part = means.at[:, my_rows, my_cols]
    zl = send(part, part, gb_s.at[0], gb_r.at[0], at_b(8))

    rz[3] = pick(3)
    gz[2] = share_z(2, rz[2])
    gx[1] = share_x(1, gz[1])

    zl.wait_recv()
    far_rows = pl.ds(pl.multiple_of((rq + 2) % 4 * Q, Q), Q)
    gy = []
    for d in range(1, 4):
        t = (c, b // 8 * 8 + (b % 8 + 2 * d) % 8)
        for i, rows in enumerate((my_rows, far_rows)):
            part = means.at[:, rows, my_cols]
            gy.append(send(part, part, gb_s.at[2 * d + i], gb_r.at[2 * d + i], t))

    fx[0] = pass_x(0, gx[0])
    gz[3] = share_z(3, rz[3])
    gx[2] = share_x(2, gz[2])
    fx[1] = pass_x(1, gx[1])

    for cp in gy:
        cp.wait_recv()
    core = b % 2
    gk = []
    for i in range(2):
        part = means.at[:, :, pl.ds(pl.multiple_of((2 * i + core) * Q, Q), Q)]
        gk.append(send(part, part, gb_s.at[8 + i], gb_r.at[8 + i], (c, b // 2 * 2 + (b + 1) % 2)))

    gx[3] = share_x(3, gz[3])
    fx[2] = pass_x(2, gx[2])
    fx[3] = pass_x(3, gx[3])
    for cp in gk:
        cp.wait_recv()
    for q in range(PLANES):
        for cp in fx[q]:
            cp.wait_recv()
    for q in range(PLANES):
        pending += a_cp[q] + rz[q] + gz[q] + gx[q] + fx[q]
    for cp in pending + rb + rc + gc + [zl] + gy + gk:
        cp.wait_send()


def multiply_kernel(offset, spec, gath, means_own, means_panel, out, normed, scale):
    p, f = pl.program_id(0), pl.program_id(1)

    @pl.when(p == 0)
    def _():
        own = lax.rsqrt(means_own[0].astype(F32))
        re = (spec[0, 0].astype(F32) * own).astype(BF16)
        im = (spec[0, 1].astype(F32) * own).astype(BF16)
        normed[f, :ROWS, :WIN] = re
        normed[f, :ROWS, WIN:] = im
        normed[f, ROWS:, :WIN] = im
        normed[f, ROWS:, WIN:] = -re

    @pl.when(f == 0)
    def _():
        here = lax.broadcasted_iota(jnp.int32, (PANEL, ROWS), 1)
        want = lax.broadcasted_iota(jnp.int32, (PANEL, ROWS), 0) + offset[p]
        onehot = jnp.where(here == want, 1.0, 0.0).astype(BF16)
        scale[...] = lax.rsqrt(jnp.dot(onehot, means_panel[0], preferred_element_type=F32))

    right = jnp.concatenate([(gath[0, 0, k].astype(F32) * scale[...]).astype(BF16) for k in range(2)], axis=1)
    for k in range(2):
        gram = lax.dot_general(
            normed[f, k * ROWS : (k + 1) * ROWS, :], right, (((1,), (1,)), ((), ())), preferred_element_type=F32
        )
        out[0, 0, k] = (gram * WIN ** (-0.5)).astype(BF16)


def local(spectra, half_width, panel_block, panel_offset):
    dma = pltpu.SemaphoreType.DMA
    vmem = pl.BlockSpec(memory_space=pltpu.VMEM)
    smem = pl.BlockSpec(memory_space=pltpu.SMEM)
    gath, means = pl.pallas_call(
        move_kernel,
        out_shape=(
            jax.ShapeDtypeStruct((2, NPANEL, 2, PANEL, WIN), BF16),
            jax.ShapeDtypeStruct((1 + NPANEL, ROWS, WIN), BF16),
        ),
        in_specs=[vmem, vmem, smem, smem],
        out_specs=(vmem, vmem),
        scratch_shapes=[pltpu.VMEM((NX, ROWS, Q), BF16)] * 4
        + [pltpu.VMEM((NZ, NPANEL, 64, Q), BF16)] * 4
        + [
            pltpu.VMEM((PLANES, NPANEL, PANEL, Q), BF16),
            pltpu.VMEM((NPANEL, PANEL, ROWS), BF16),
            pltpu.VMEM((ROWS + 2 * HALO, WIN), BF16),
            pltpu.VMEM((NBAND, Q + 2 * HALO, Q), BF16),
            pltpu.VMEM((Q + 2 * HALO, Q), F32),
            pltpu.VMEM((Q, Q), F32),
            pltpu.VMEM((NCHAN, 8, Q), F32),
            pltpu.VMEM((32, Q), BF16),
            pltpu.VMEM((NCHAN, 32, Q), BF16),
        ]
        + [dma((4, 4))] * 8
        + [dma((2,))] * 2
        + [dma((16,))] * 6
        + [dma((10,))] * 2,
        compiler_params=pltpu.CompilerParams(
            collective_id=0, has_side_effects=True, vmem_limit_bytes=40 * 1024 * 1024
        ),
        name="move_panels_and_power",
    )(spectra, half_width[None, :], panel_block, panel_offset)
    return pl.pallas_call(
        multiply_kernel,
        out_shape=jax.ShapeDtypeStruct((NPANEL, 2, 2, ROWS, PANEL), BF16),
        grid=(NPANEL, 2),
        in_specs=[
            smem,
            pl.BlockSpec((1, 2, ROWS, WIN), lambda p, f: (jnp.where(p == 0, f, 1), 0, 0, 0)),
            pl.BlockSpec((1, 1, 2, PANEL, WIN), lambda p, f: (f, p, 0, 0, 0)),
            pl.BlockSpec((1, ROWS, WIN), lambda p, f: (0, 0, 0)),
            pl.BlockSpec((1, ROWS, WIN), lambda p, f: (1 + p, 0, 0)),
        ],
        out_specs=pl.BlockSpec((1, 1, 2, ROWS, PANEL), lambda p, f: (p, f, 0, 0, 0)),
        scratch_shapes=[pltpu.VMEM((2, 2 * ROWS, 2 * WIN), BF16), pltpu.VMEM((PANEL, WIN), F32)],
        compiler_params=pltpu.CompilerParams(vmem_limit_bytes=40 * 1024 * 1024),
        name="normalize_and_multiply",
    )(panel_offset, spectra, gath, means, means)


def solution(mesh):
    placed = (P("band", None, "chan", None), P(), P(), P())
    return jax.shard_map(
        local,
        mesh=mesh,
        in_specs=placed,
        out_specs=P(None, "band", None, "chan", None),
        check_vma=False,
    )
```

```python
import jax
import jax.numpy as jnp
from jax import lax
from jax.experimental import pallas as pl
from jax.experimental.pallas import tpu as pltpu
from jax.sharding import PartitionSpec as P

MESH = pl.DeviceIdType.MESH
PANEL = 256
NPANEL = 4
HALO = 32
ROWS = 512
WIN = 512
Q = 128
R = 64
NX = 4
NZ = 4
NCHAN = 16
NBAND = 16
PLANES = 4
CHANNELS = ROWS * NCHAN
BINS = 32
WB = WIN // NBAND
F32 = jnp.float32
BF16 = jnp.bfloat16

PLAN = (
    ("pick", 0), ("pick", 2), ("band_sum", 0), ("pick", 3), ("window", 0), ("share_z", 2), ("pick", 1), ("own_y", 0),
    ("share_z", 0), ("pass_z", 2), ("share_z", 3), ("pass_z", 0), ("pick", 4), ("share_x", 2), ("choose", 0),
    ("pass_z", 3), ("own_core", 0), ("share_z", 1), ("share_x", 0), ("gathered", 0), ("pick", 6), ("share_z", 4),
    ("share_x", 3), ("pass_z", 1), ("pass_x", 2), ("pass_x", 3), ("panel_y", 0), ("share_z", 6), ("pass_x", 0),
    ("pass_z", 4), ("pick", 7), ("share_x", 1), ("share_x", 4), ("pass_z", 6), ("pick", 5), ("own_norm", 0),
    ("panel_core", 0), ("share_z", 7), ("share_x", 6), ("pass_x", 1), ("share_z", 5), ("pass_x", 4), ("pass_z", 7),
    ("own_norm", 1), ("pass_x", 6), ("pass_z", 5), ("share_x", 7), ("panel_scale", 0), ("share_x", 5),
    ("multiply", 2), ("pass_x", 7), ("multiply", 1), ("pass_x", 5), ("multiply", 0), ("multiply", 3),
)


def root(fourth):
    return lax.rsqrt(jnp.sqrt(jnp.sqrt(fourth)))


def move_kernel(
    spec_hbm, width_hbm, block_hbm, offset_hbm, out_hbm,
    spec, width, block, offset, a0, a1, a2, a3, b0, b1, b2, b3, b4, b5, b6, b7, gath, picked, onehot, power, bands, total,
    cand, parts, means, scale, left, out, l_s, o_s, a_s, a_r, rz_s, rz_r, gz_s, gz_r, gx_s, gx_r, e_s, e_r, rb_s, rb_r, rc_s, rc_r, gc_s, gc_r, gb_s, gb_r,
):
    c, b = lax.axis_index("chan"), lax.axis_index("band")
    x, z = c // NZ, c % NZ
    core = b % 2
    half_band = b // 2
    wb = core * 8 + half_band
    a, zb = (a0, a1, a2, a3), (b0, b1, b2, b3, b4, b5, b6, b7)

    def at_x(d):
        return ((x + d) % NX * NZ + z, b)

    def at_z(d):
        return (x * NZ + (z + d) % NZ, b)

    def at_c(d):
        return ((c + d) % NCHAN, b)

    def at_b(d):
        return (c, (b + d) % NBAND)

    def block_of(i, size, count=None):
        return pl.ds(pl.multiple_of(i * size, size), count or size)

    def send(src, dst, ssem, rsem, dev):
        copy = pltpu.make_async_remote_copy(
            src_ref=src, dst_ref=dst, send_sem=ssem, recv_sem=rsem, device_id=dev, device_id_type=MESH
        )
        copy.start()
        return copy

    loads = [
        pltpu.make_async_copy(src, dst, l_s.at[i])
        for i, (src, dst) in enumerate(
            ((spec_hbm, spec), (width_hbm, width), (block_hbm, block), (offset_hbm, offset))
        )
    ]
    for cp in loads:
        cp.start()
    barrier = pltpu.get_barrier_semaphore()
    for d in range(1, NCHAN):
        pl.semaphore_signal(barrier, inc=1, device_id=at_c(d), device_id_type=MESH)
    for d in range(1, NBAND):
        pl.semaphore_signal(barrier, inc=1, device_id=at_b(d), device_id_type=MESH)
    pl.semaphore_wait(barrier, NCHAN + NBAND - 2)

    a_cp = [None] * PLANES
    for q in range(PLANES):
        f, k = q // 2, q % 2
        a_cp[q] = []
        for d in (1, 3, 2):
            cols = block_of((x + d) % NX, Q)
            a_cp[q].append(send(spec_hbm.at[f, k, :, cols], a[q].at[d], a_s.at[q, d], a_r.at[q, d], at_x(d)))

    for cp in loads:
        cp.wait()
    for i in range(ROWS // Q):
        acc = jnp.zeros((Q, WIN), F32)
        for f in range(2):
            for k in range(2):
                v = spec[f, k, i * Q : (i + 1) * Q, :].astype(F32)
                acc = acc + v * v
        for j in range(WIN // Q):
            power[j * Q : (j + 1) * Q, i * Q : (i + 1) * Q] = acc[:, j * Q : (j + 1) * Q].T.astype(BF16)
    rb = []
    for d in range(1, NBAND):
        t = (b + d) % NBAND
        src = power.at[block_of(t % 2 * 8 + t // 2, WB), :]
        rb.append(send(src, bands.at[d], rb_s.at[d], rb_r.at[d], at_b(d)))

    for q in range(PLANES):
        a[q][0] = spec[q // 2, q % 2, :, block_of(x, Q)]
    for p in range(NPANEL):
        here = lax.broadcasted_iota(jnp.int32, (PANEL, ROWS), 1)
        want = lax.broadcasted_iota(jnp.int32, (PANEL, ROWS), 0) + offset[p]
        onehot[p] = jnp.where(here == want, 1.0, 0.0).astype(BF16)

    st = {"rb": rb}

    def wait(name):
        for cp in st[name]:
            cp.wait_recv()

    arrived = set()

    def pick(u):
        q, h = u // 2, u % 2
        if q not in arrived:
            arrived.add(q)
            for cp in a_cp[q]:
                cp.wait_recv()
        for p in (2 * h, 2 * h + 1):
            slot = lax.rem(x - block[p] // NZ + NX, NX)
            picked[q, p] = jnp.dot(onehot[p], a[q][slot], preferred_element_type=F32).astype(BF16)
        zb[u][0] = picked[q, 2 * h : 2 * h + 2, block_of(z, R), :]
        st["rz", u] = []
        for d in (1, 3, 2):
            src = picked.at[q, pl.ds(2 * h, 2), block_of((z + d) % NZ, R), :]
            st["rz", u].append(send(src, zb[u].at[d], rz_s.at[u, d], rz_r.at[u, d], at_z(d)))

    def share_z(u):
        q, h = u // 2, u % 2
        wait(("rz", u))
        for i in range(2):
            slot = lax.rem(z - block[2 * h + i] % NZ + NZ, NZ)
            gath[q // 2, 2 * h + i, q % 2, block_of(z, R), block_of(x, Q)] = zb[u][slot, i]
        part = gath.at[q // 2, pl.ds(2 * h, 2), q % 2, block_of(z, R), block_of(x, Q)]
        st["gz", u] = [send(part, part, gz_s.at[u, i], gz_r.at[u, i], at_z(d)) for i, d in enumerate((1, 3))]

    def pass_z(u):
        q, h = u // 2, u % 2
        st["fz", u] = []
        for i, (came, to) in enumerate(((3, 1), (1, 3))):
            st["gz", u][i].wait_recv()
            part = gath.at[q // 2, 2 * h + i, q % 2, block_of((z + came) % NZ, R), block_of(x, Q)]
            st["fz", u].append(send(part, part, gz_s.at[u, 2 + i], gz_r.at[u, 2 + i], at_z(to)))

    def share_x(u):
        q, h = u // 2, u % 2
        wait(("fz", u))
        part = gath.at[q // 2, pl.ds(2 * h, 2), q % 2, :, block_of(x, Q)]
        st["gx", u] = [send(part, part, gx_s.at[u, i], gx_r.at[u, i], at_x(d)) for i, d in enumerate((1, 3))]

    def pass_x(u):
        q, h = u // 2, u % 2
        st["fx", u] = []
        for i, (came, to) in enumerate(((3, 1), (1, 3))):
            st["gx", u][i].wait_recv()
            part = gath.at[q // 2, 2 * h + i, q % 2, :, block_of((x + came) % NX, Q)]
            st["fx", u].append(send(part, part, gx_s.at[u, 2 + i], gx_r.at[u, 2 + i], at_x(to)))

    mine = block_of(wb, WB)
    across = block_of(core * 8 + (half_band + 4) % 8, WB)
    own_lanes, panel_lanes = pl.ds(0, ROWS), pl.ds(ROWS, NPANEL * PANEL)

    def band_sum(_):
        wait("rb")
        acc = power[mine, :].astype(F32)
        for d in range(1, NBAND):
            acc = acc + bands[d].astype(F32)
        total[:, Q : Q + ROWS] = acc
        st["e"] = [
            send(total.at[:, pl.ds(ROWS, Q)], total.at[:, pl.ds(0, Q)], e_s.at[0], e_r.at[0], at_c(1)),
            send(total.at[:, pl.ds(Q, Q)], total.at[:, pl.ds(ROWS + Q, Q)], e_s.at[1], e_r.at[1], at_c(NCHAN - 1)),
        ]

    def window(_):
        wait("e")
        wide = ROWS + 2 * Q
        chan = lax.broadcasted_iota(jnp.int32, (WB, wide), 1) + (c * ROWS - Q)
        ext = jnp.where((chan >= 0) & (chan < CHANNELS), total[...], 0.0)
        row = lax.broadcasted_iota(jnp.int32, (WB, ROWS), 0)
        half = jnp.zeros((WB, ROWS), jnp.int32)
        for i in range(WB):
            half = jnp.where(row == i, width[wb * WB + i], half)
        win = ext[:, Q : Q + ROWS]
        for o in range(1, HALO + 1):
            both = pltpu.roll(ext, o, 1) + pltpu.roll(ext, wide - o, 1)
            win = win + jnp.where(half >= o, both[:, Q : Q + ROWS], 0.0)
        chan = lax.broadcasted_iota(jnp.int32, (WB, ROWS), 1) + c * ROWS
        count = jnp.minimum(chan + half, CHANNELS - 1) - jnp.maximum(chan - half, 0) + 1
        mean = win / (count.astype(F32) * BINS) + 1e-6
        mean = ((mean * mean) * (mean * mean)).astype(BF16)
        means[mine, own_lanes] = mean
        part = means.at[mine, own_lanes]
        st["oz"] = [send(part, part, gb_s.at[0], gb_r.at[0], at_b(8))]
        for p in range(NPANEL):
            cand[:, p * PANEL : (p + 1) * PANEL] = lax.dot_general(
                mean, onehot[p], (((1,), (1,)), ((), ())), preferred_element_type=F32
            ).astype(BF16)
        st["rc"] = []
        for d in range(1, NCHAN):
            t = (c + d) % NCHAN
            src = cand.at[block_of(t % 2, 16), block_of(t // 2, Q)]
            st["rc"].append(send(src, parts.at[d], rc_s.at[d], rc_r.at[d], at_c(d)))
        parts[0] = cand[block_of(c % 2, 16), block_of(c // 2, Q)]

    def choose(_):
        wait("rc")
        mine_too = means.at[pl.ds(pl.multiple_of(wb * WB + c % 2 * 16, 16), 16), pl.ds(pl.multiple_of(ROWS + c // 2 * Q, Q), Q)]
        mine_too[...] = parts[lax.rem(c - block[c // 4] + NCHAN, NCHAN)]
        st["gc"] = [send(mine_too, mine_too, gc_s.at[d], gc_r.at[d], at_c(d)) for d in range(1, NCHAN)]

    def gathered(_):
        wait("gc")
        part = means.at[mine, panel_lanes]
        st["pz"] = [send(part, part, gb_s.at[8], gb_r.at[8], at_b(8))]

    def along_y(here, there, lanes, sem):
        wait(here)
        st[there] = []
        for d in range(1, 4):
            t = (c, b // 8 * 8 + (b % 8 + 2 * d) % 8)
            for i, rows in enumerate((mine, across)):
                part = means.at[rows, lanes]
                s = sem + 2 * d - 1 + i
                st[there].append(send(part, part, gb_s.at[s], gb_r.at[s], t))

    def to_core(here, there, lanes, sem):
        wait(here)
        part = means.at[block_of(core, WIN // 2), lanes]
        st[there] = [send(part, part, gb_s.at[sem], gb_r.at[sem], (c, half_band * 2 + (core + 1) % 2))]

    def own_norm(half):
        if half == 0:
            wait("ok")
        for i in range(2 * half, 2 * half + 2):
            for j in range(WIN // Q):
                s = root(means[j * Q : (j + 1) * Q, i * Q : (i + 1) * Q].astype(F32)).T
                for f in range(2):
                    for k in range(2):
                        v = spec[f, k, i * Q : (i + 1) * Q, j * Q : (j + 1) * Q].astype(F32)
                        left[f, i * Q : (i + 1) * Q, k * WIN + j * Q : k * WIN + (j + 1) * Q] = (v * s).astype(BF16)

    def panel_scale(_):
        wait("pk")
        for p in range(NPANEL):
            for i in range(PANEL // Q):
                lanes = slice(ROWS + p * PANEL + i * Q, ROWS + p * PANEL + (i + 1) * Q)
                for j in range(WIN // Q):
                    scale[p, i * Q : (i + 1) * Q, j * Q : (j + 1) * Q] = root(
                        means[j * Q : (j + 1) * Q, lanes].astype(F32)
                    ).T

    stores = []

    def multiply(v):
        f, h = v // 2, v % 2
        wait(("fx", 4 * f + h))
        wait(("fx", 4 * f + 2 + h))

        def body(p, carry):
            re = (gath[f, p, 0].astype(F32) * scale[p]).astype(BF16)
            im = (gath[f, p, 1].astype(F32) * scale[p]).astype(BF16)
            for k, right in enumerate((jnp.concatenate([re, im], axis=1), jnp.concatenate([-im, re], axis=1))):
                gram = lax.dot_general(left[f], right, (((1,), (1,)), ((), ())), preferred_element_type=F32)
                out[p, f, k] = (gram * WIN ** (-0.5)).astype(BF16)
            return carry

        lax.fori_loop(2 * h, 2 * h + 2, body, 0)
        stores.append(pltpu.make_async_copy(out.at[pl.ds(2 * h, 2), f], out_hbm.at[pl.ds(2 * h, 2), f], o_s.at[v]))
        stores[-1].start()

    steps = {
        "pick": pick, "share_z": share_z, "pass_z": pass_z, "share_x": share_x, "pass_x": pass_x, "multiply": multiply,
        "band_sum": band_sum, "window": window, "choose": choose, "gathered": gathered,
        "own_y": lambda _: along_y("oz", "oy", own_lanes, 0),
        "own_core": lambda _: to_core("oy", "ok", own_lanes, 7),
        "panel_y": lambda _: along_y("pz", "py", panel_lanes, 8),
        "panel_core": lambda _: to_core("py", "pk", panel_lanes, 15),
        "own_norm": own_norm, "panel_scale": panel_scale,
    }
    for name, q in PLAN:
        steps[name](q)
    for group in a_cp + list(st.values()):
        for cp in group:
            cp.wait_send()
    for cp in stores:
        cp.wait()


def local(spectra, half_width, panel_block, panel_offset):
    dma = pltpu.SemaphoreType.DMA
    hbm = pl.BlockSpec(memory_space=pltpu.HBM)
    return pl.pallas_call(
        move_kernel,
        out_shape=jax.ShapeDtypeStruct((NPANEL, 2, 2, ROWS, PANEL), BF16),
        in_specs=[hbm] * 4,
        out_specs=hbm,
        scratch_shapes=[
            pltpu.VMEM((2, 2, ROWS, WIN), BF16),
            pltpu.SMEM((WIN,), jnp.int32),
            pltpu.SMEM((NPANEL,), jnp.int32),
            pltpu.SMEM((NPANEL,), jnp.int32),
        ]
        + [pltpu.VMEM((NX, ROWS, Q), BF16)] * 4
        + [pltpu.VMEM((NZ, 2, R, Q), BF16)] * 8
        + [
            pltpu.VMEM((2, NPANEL, 2, PANEL, WIN), BF16),
            pltpu.VMEM((PLANES, NPANEL, PANEL, Q), BF16),
            pltpu.VMEM((NPANEL, PANEL, ROWS), BF16),
            pltpu.VMEM((WIN, ROWS), BF16),
            pltpu.VMEM((NBAND, WB, ROWS), BF16),
            pltpu.VMEM((WB, ROWS + 2 * Q), F32),
            pltpu.VMEM((WB, NPANEL * PANEL), BF16),
            pltpu.VMEM((NCHAN, 16, Q), BF16),
            pltpu.VMEM((WIN, ROWS + NPANEL * PANEL), BF16),
            pltpu.VMEM((NPANEL, PANEL, WIN), F32),
            pltpu.VMEM((2, ROWS, 2 * WIN), BF16),
            pltpu.VMEM((NPANEL, 2, 2, ROWS, PANEL), BF16),
            dma((4,)),
            dma((4,)),
        ]
        + [dma((4, 4))] * 2
        + [dma((8, 4))] * 6
        + [dma((2,))] * 2
        + [dma((16,))] * 8,
        compiler_params=pltpu.CompilerParams(
            collective_id=0, has_side_effects=True, vmem_limit_bytes=60 * 1024 * 1024
        ),
        name="cross_spectra",
    )(spectra, half_width, panel_block, panel_offset)


def solution(mesh):
    placed = (P("band", None, "chan", None), P(), P(), P())
    return jax.shard_map(
        local,
        mesh=mesh,
        in_specs=placed,
        out_specs=P(None, "band", None, "chan", None),
        check_vma=False,
    )
```

```python
import jax
import jax.numpy as jnp
from jax import lax
from jax.experimental import pallas as pl
from jax.experimental.pallas import tpu as pltpu
from jax.sharding import PartitionSpec as P

MESH = pl.DeviceIdType.MESH
PANEL = 256
NPANEL = 4
HALO = 32
ROWS = 512
WIN = 512
Q = 128
R = 64
NX = 4
NZ = 4
NCHAN = 16
NBAND = 16
PLANES = 4
CHANNELS = ROWS * NCHAN
BINS = 32
WB = WIN // NBAND
F32 = jnp.float32
BF16 = jnp.bfloat16

PLAN = (
    ("raw", 0), ("power", 0), ("prepare", 0), ("pick", 1), ("raw", 3), ("band_sum", 0), ("pick", 0), ("raw", 1),
    ("raw", 2), ("share_z", 1), ("pick", 6), ("window", 0), ("pass_z", 1), ("pick", 2), ("share_z", 0),
    ("share_z", 6), ("share_x", 1), ("share_z", 2), ("pick", 4), ("pass_z", 6), ("pass_x", 1), ("choose", 0),
    ("pass_z", 0), ("own_y", 0), ("share_z", 4), ("pass_z", 2), ("share_x", 6), ("gathered", 0), ("pick", 7),
    ("share_x", 0), ("panel_y", 0), ("pass_z", 4), ("share_x", 2), ("pick", 3), ("share_z", 7),
    ("share_x", 4), ("pick", 5), ("pass_x", 2), ("pass_x", 6), ("panel_core", 0), ("pass_x", 0), ("pass_z", 7),
    ("own_core", 0), ("share_z", 3), ("share_z", 5), ("pass_x", 4), ("share_x", 7), ("pass_z", 3), ("panel_scale", 0),
    ("pass_z", 5), ("share_x", 3), ("own_norm", 0), ("share_x", 5), ("own_norm", 1), ("multiply", 2), ("pass_x", 3),
    ("pass_x", 7), ("multiply", 0), ("pass_x", 5), ("multiply", 1), ("multiply", 3),
)


def root(fourth):
    return lax.rsqrt(jnp.sqrt(jnp.sqrt(fourth)))


def move_kernel(
    spec_hbm, width_hbm, block_hbm, offset_hbm, out_hbm,
    spec, width, block, offset, a0, a1, a2, a3, b0, b1, b2, b3, b4, b5, b6, b7, gath, picked, onehot, power, bands, total,
    cand, parts, means, scale, left, out, l_s, o_s, a_s, a_r, rz_s, rz_r, gz_s, gz_r, gx_s, gx_r, e_s, e_r, rb_s, rb_r, rc_s, rc_r, gc_s, gc_r, gb_s, gb_r,
):
    c, b = lax.axis_index("chan"), lax.axis_index("band")
    x, z = c // NZ, c % NZ
    core = b % 2
    half_band = b // 2

    def windows_of(t):
        return t % 2 * 8 + t // 2 % 4 * 2 + t // 8

    wb = windows_of(b)
    a, zb = (a0, a1, a2, a3), (b0, b1, b2, b3, b4, b5, b6, b7)

    def at_x(d):
        return ((x + d) % NX * NZ + z, b)

    def at_z(d):
        return (x * NZ + (z + d) % NZ, b)

    def at_c(d):
        return ((c + d) % NCHAN, b)

    def at_b(d):
        return (c, (b + d) % NBAND)

    def block_of(i, size, count=None):
        return pl.ds(pl.multiple_of(i * size, size), count or size)

    def send(src, dst, ssem, rsem, dev):
        copy = pltpu.make_async_remote_copy(
            src_ref=src, dst_ref=dst, send_sem=ssem, recv_sem=rsem, device_id=dev, device_id_type=MESH
        )
        copy.start()
        return copy

    loads = [
        pltpu.make_async_copy(src, dst, l_s.at[i])
        for i, (src, dst) in enumerate(
            ((spec_hbm, spec), (width_hbm, width), (block_hbm, block), (offset_hbm, offset))
        )
    ]
    for cp in loads:
        cp.start()
    barrier = pltpu.get_barrier_semaphore()
    for d in range(1, NCHAN):
        pl.semaphore_signal(barrier, inc=1, device_id=at_c(d), device_id_type=MESH)
    for d in range(1, NBAND):
        pl.semaphore_signal(barrier, inc=1, device_id=at_b(d), device_id_type=MESH)
    pl.semaphore_wait(barrier, NCHAN + NBAND - 2)

    a_cp = [None] * PLANES

    def raw(q):
        a_cp[q] = []
        for d in (1, 3, 2):
            src = spec_hbm.at[q // 2, q % 2, :, block_of((x + d) % NX, Q)]
            a_cp[q].append(send(src, a[q].at[d], a_s.at[q, d], a_r.at[q, d], at_x(d)))

    def own_power(_):
        for cp in loads:
            cp.wait()
        for i in range(ROWS // Q):
            acc = jnp.zeros((Q, WIN), F32)
            for f in range(2):
                for k in range(2):
                    v = spec[f, k, i * Q : (i + 1) * Q, :].astype(F32)
                    acc = acc + v * v
            for j in range(WIN // Q):
                power[j * Q : (j + 1) * Q, i * Q : (i + 1) * Q] = acc[:, j * Q : (j + 1) * Q].T.astype(BF16)
        st["rb"] = []
        for d in range(1, NBAND):
            src = power.at[block_of(windows_of((b + d) % NBAND), WB), :]
            st["rb"].append(send(src, bands.at[d], rb_s.at[d], rb_r.at[d], at_b(d)))

    def prepare(_):
        for q in range(PLANES):
            a[q][0] = spec[q // 2, q % 2, :, block_of(x, Q)]
        for p in range(NPANEL):
            here = lax.broadcasted_iota(jnp.int32, (PANEL, ROWS), 1)
            want = lax.broadcasted_iota(jnp.int32, (PANEL, ROWS), 0) + offset[p]
            onehot[p] = jnp.where(here == want, 1.0, 0.0).astype(BF16)

    st = {}

    def wait(name):
        for cp in st[name]:
            cp.wait_recv()

    arrived = set()

    def pick(u):
        q, h = u // 2, u % 2
        if q not in arrived:
            arrived.add(q)
            for cp in a_cp[q]:
                cp.wait_recv()
        for p in (2 * h, 2 * h + 1):
            slot = lax.rem(x - block[p] // NZ + NX, NX)
            picked[q, p] = jnp.dot(onehot[p], a[q][slot], preferred_element_type=F32).astype(BF16)
        zb[u][0] = picked[q, 2 * h : 2 * h + 2, block_of(z, R), :]
        st["rz", u] = []
        for d in (1, 3, 2):
            src = picked.at[q, pl.ds(2 * h, 2), block_of((z + d) % NZ, R), :]
            st["rz", u].append(send(src, zb[u].at[d], rz_s.at[u, d], rz_r.at[u, d], at_z(d)))

    def share_z(u):
        q, h = u // 2, u % 2
        wait(("rz", u))
        for i in range(2):
            slot = lax.rem(z - block[2 * h + i] % NZ + NZ, NZ)
            gath[q // 2, 2 * h + i, q % 2, block_of(z, R), block_of(x, Q)] = zb[u][slot, i]
        part = gath.at[q // 2, pl.ds(2 * h, 2), q % 2, block_of(z, R), block_of(x, Q)]
        st["gz", u] = [send(part, part, gz_s.at[u, i], gz_r.at[u, i], at_z(d)) for i, d in enumerate((1, 3))]

    def pass_z(u):
        q, h = u // 2, u % 2
        st["fz", u] = []
        for i, (came, to) in enumerate(((3, 1), (1, 3))):
            st["gz", u][i].wait_recv()
            part = gath.at[q // 2, 2 * h + i, q % 2, block_of((z + came) % NZ, R), block_of(x, Q)]
            st["fz", u].append(send(part, part, gz_s.at[u, 2 + i], gz_r.at[u, 2 + i], at_z(to)))

    def share_x(u):
        q, h = u // 2, u % 2
        wait(("fz", u))
        part = gath.at[q // 2, pl.ds(2 * h, 2), q % 2, :, block_of(x, Q)]
        st["gx", u] = [send(part, part, gx_s.at[u, i], gx_r.at[u, i], at_x(d)) for i, d in enumerate((1, 3))]

    def pass_x(u):
        q, h = u // 2, u % 2
        st["fx", u] = []
        for i, (came, to) in enumerate(((3, 1), (1, 3))):
            st["gx", u][i].wait_recv()
            part = gath.at[q // 2, 2 * h + i, q % 2, :, block_of((x + came) % NX, Q)]
            st["fx", u].append(send(part, part, gx_s.at[u, 2 + i], gx_r.at[u, 2 + i], at_x(to)))

    mine = block_of(wb, WB)
    pair = block_of(wb // 2, 2 * WB)
    own_lanes, panel_lanes = pl.ds(0, ROWS), pl.ds(ROWS, NPANEL * PANEL)

    def band_sum(_):
        wait("rb")
        acc = power[mine, :].astype(F32)
        for d in range(1, NBAND):
            acc = acc + bands[d].astype(F32)
        total[:, Q : Q + ROWS] = acc
        st["e"] = [
            send(total.at[:, pl.ds(ROWS, Q)], total.at[:, pl.ds(0, Q)], e_s.at[0], e_r.at[0], at_c(1)),
            send(total.at[:, pl.ds(Q, Q)], total.at[:, pl.ds(ROWS + Q, Q)], e_s.at[1], e_r.at[1], at_c(15)),
        ]

    def window(_):
        wait("e")
        wide = ROWS + 2 * Q
        chan = lax.broadcasted_iota(jnp.int32, (WB, wide), 1) + (c * ROWS - Q)
        ext = jnp.where((chan >= 0) & (chan < CHANNELS), total[...], 0.0)
        row = lax.broadcasted_iota(jnp.int32, (WB, ROWS), 0)
        half = jnp.zeros((WB, ROWS), jnp.int32)
        for i in range(WB):
            half = jnp.where(row == i, width[wb * WB + i], half)
        win = ext[:, Q : Q + ROWS]
        for o in range(1, HALO + 1):
            both = pltpu.roll(ext, o, 1) + pltpu.roll(ext, wide - o, 1)
            win = win + jnp.where(half >= o, both[:, Q : Q + ROWS], 0.0)
        chan = lax.broadcasted_iota(jnp.int32, (WB, ROWS), 1) + c * ROWS
        count = jnp.minimum(chan + half, CHANNELS - 1) - jnp.maximum(chan - half, 0) + 1
        mean = win / (count.astype(F32) * BINS) + 1e-6
        mean = ((mean * mean) * (mean * mean)).astype(BF16)
        means[mine, own_lanes] = mean
        part = means.at[mine, own_lanes]
        st["oz"] = [send(part, part, gb_s.at[0], gb_r.at[0], at_b(8))]
        for p in range(NPANEL):
            cand[:, p * PANEL : (p + 1) * PANEL] = lax.dot_general(
                mean, onehot[p], (((1,), (1,)), ((), ())), preferred_element_type=F32
            ).astype(BF16)
        st["rc"] = []
        for d in range(1, NCHAN):
            t = (c + d) % NCHAN
            src = cand.at[block_of(t % 2, 16), block_of(t // 2, Q)]
            st["rc"].append(send(src, parts.at[d], rc_s.at[d], rc_r.at[d], at_c(d)))
        parts[0] = cand[block_of(c % 2, 16), block_of(c // 2, Q)]

    def choose(_):
        wait("rc")
        mine_too = means.at[pl.ds(pl.multiple_of(wb * WB + c % 2 * 16, 16), 16), pl.ds(pl.multiple_of(ROWS + c // 2 * Q, Q), Q)]
        mine_too[...] = parts[lax.rem(c - block[c // 4] + NCHAN, NCHAN)]
        st["gc"] = [send(mine_too, mine_too, gc_s.at[d], gc_r.at[d], at_c(d)) for d in range(1, NCHAN)]

    def gathered(_):
        wait("gc")
        part = means.at[mine, panel_lanes]
        st["pz"] = [send(part, part, gb_s.at[8], gb_r.at[8], at_b(8))]

    def along_y(here, there, lanes, sem):
        wait(here)
        st[there] = []
        for d in range(1, 4):
            t = (c, b // 8 * 8 + (b % 8 + 2 * d) % 8)
            part = means.at[pair, lanes]
            st[there].append(send(part, part, gb_s.at[sem + d], gb_r.at[sem + d], t))

    def to_core(here, there, lanes, sem):
        wait(here)
        part = means.at[block_of(core, WIN // 2), lanes]
        st[there] = [send(part, part, gb_s.at[sem], gb_r.at[sem], (c, half_band * 2 + (core + 1) % 2))]

    def own_norm(half):
        if half == 0:
            wait("ok")
        for i in range(2 * half, 2 * half + 2):
            for j in range(WIN // Q):
                s = root(means[j * Q : (j + 1) * Q, i * Q : (i + 1) * Q].astype(F32)).T
                for f in range(2):
                    for k in range(2):
                        v = spec[f, k, i * Q : (i + 1) * Q, j * Q : (j + 1) * Q].astype(F32)
                        left[f, i * Q : (i + 1) * Q, k * WIN + j * Q : k * WIN + (j + 1) * Q] = (v * s).astype(BF16)

    def panel_scale(_):
        wait("pk")
        for p in range(NPANEL):
            for i in range(PANEL // Q):
                lanes = slice(ROWS + p * PANEL + i * Q, ROWS + p * PANEL + (i + 1) * Q)
                for j in range(WIN // Q):
                    scale[p, i * Q : (i + 1) * Q, j * Q : (j + 1) * Q] = root(
                        means[j * Q : (j + 1) * Q, lanes].astype(F32)
                    ).T

    stores = []

    def multiply(v):
        f, h = v // 2, v % 2
        wait(("fx", 4 * f + h))
        wait(("fx", 4 * f + 2 + h))

        def body(p, carry):
            re = (gath[f, p, 0].astype(F32) * scale[p]).astype(BF16)
            im = (gath[f, p, 1].astype(F32) * scale[p]).astype(BF16)
            for k, right in enumerate((jnp.concatenate([re, im], axis=1), jnp.concatenate([-im, re], axis=1))):
                gram = lax.dot_general(left[f], right, (((1,), (1,)), ((), ())), preferred_element_type=F32)
                out[p, f, k] = (gram * WIN ** (-0.5)).astype(BF16)
            return carry

        lax.fori_loop(2 * h, 2 * h + 2, body, 0)
        stores.append(pltpu.make_async_copy(out.at[pl.ds(2 * h, 2), f], out_hbm.at[pl.ds(2 * h, 2), f], o_s.at[v]))
        stores[-1].start()

    steps = {
        "raw": raw, "power": own_power, "prepare": prepare,
        "pick": pick, "share_z": share_z, "pass_z": pass_z, "share_x": share_x, "pass_x": pass_x, "multiply": multiply,
        "band_sum": band_sum, "window": window, "choose": choose, "gathered": gathered,
        "own_y": lambda _: along_y("oz", "oy", own_lanes, 0),
        "own_core": lambda _: to_core("oy", "ok", own_lanes, 7),
        "panel_y": lambda _: along_y("pz", "py", panel_lanes, 8),
        "panel_core": lambda _: to_core("py", "pk", panel_lanes, 15),
        "own_norm": own_norm, "panel_scale": panel_scale,
    }
    for name, q in PLAN:
        steps[name](q)
    for group in a_cp + list(st.values()):
        for cp in group:
            cp.wait_send()
    for cp in stores:
        cp.wait()


def deliver_kernel(src, dst, held, in_sem, out_sem):
    pieces = [(p, f, k) for p in range(NPANEL) for f in range(2) for k in range(2)]
    come = [pltpu.make_async_copy(src.at[i], held.at[i], in_sem.at[n]) for n, i in enumerate(pieces)]
    go = [pltpu.make_async_copy(held.at[i], dst.at[i], out_sem.at[n]) for n, i in enumerate(pieces)]
    for cp in come:
        cp.start()
    for one, two in zip(come, go):
        one.wait()
        two.start()
    for cp in go:
        cp.wait()


def local(spectra, half_width, panel_block, panel_offset):
    dma = pltpu.SemaphoreType.DMA
    hbm = pl.BlockSpec(memory_space=pltpu.HBM)
    products = pl.pallas_call(
        move_kernel,
        out_shape=jax.ShapeDtypeStruct((NPANEL, 2, 2, ROWS, PANEL), BF16),
        in_specs=[hbm] * 4,
        out_specs=hbm,
        scratch_shapes=[
            pltpu.VMEM((2, 2, ROWS, WIN), BF16),
            pltpu.SMEM((WIN,), jnp.int32),
            pltpu.SMEM((NPANEL,), jnp.int32),
            pltpu.SMEM((NPANEL,), jnp.int32),
        ]
        + [pltpu.VMEM((NX, ROWS, Q), BF16)] * 4
        + [pltpu.VMEM((NZ, 2, R, Q), BF16)] * 8
        + [
            pltpu.VMEM((2, NPANEL, 2, PANEL, WIN), BF16),
            pltpu.VMEM((PLANES, NPANEL, PANEL, Q), BF16),
            pltpu.VMEM((NPANEL, PANEL, ROWS), BF16),
            pltpu.VMEM((WIN, ROWS), BF16),
            pltpu.VMEM((NBAND, WB, ROWS), BF16),
            pltpu.VMEM((WB, ROWS + 2 * Q), F32),
            pltpu.VMEM((WB, NPANEL * PANEL), BF16),
            pltpu.VMEM((NCHAN, 16, Q), BF16),
            pltpu.VMEM((WIN, ROWS + NPANEL * PANEL), BF16),
            pltpu.VMEM((NPANEL, PANEL, WIN), F32),
            pltpu.VMEM((2, ROWS, 2 * WIN), BF16),
            pltpu.VMEM((NPANEL, 2, 2, ROWS, PANEL), BF16),
            dma((4,)),
            dma((4,)),
        ]
        + [dma((4, 4))] * 2
        + [dma((8, 4))] * 6
        + [dma((2,))] * 2
        + [dma((16,))] * 8,
        compiler_params=pltpu.CompilerParams(
            collective_id=0, has_side_effects=True, vmem_limit_bytes=60 * 1024 * 1024
        ),
        name="cross_spectra",
    )(spectra, half_width, panel_block, panel_offset)
    return pl.pallas_call(
        deliver_kernel,
        out_shape=jax.ShapeDtypeStruct(products.shape, BF16),
        in_specs=[hbm],
        out_specs=hbm,
        scratch_shapes=[pltpu.VMEM(products.shape, BF16), dma((16,)), dma((16,))],
        compiler_params=pltpu.CompilerParams(vmem_limit_bytes=60 * 1024 * 1024),
        name="deliver",
    )(products)


def solution(mesh):
    placed = (P("band", None, "chan", None), P(), P(), P())
    return jax.shard_map(
        local,
        mesh=mesh,
        in_specs=placed,
        out_specs=P(None, "band", None, "chan", None),
        check_vma=False,
    )
```

```python
import jax
import jax.numpy as jnp
from jax import lax
from jax.experimental import pallas as pl
from jax.experimental.pallas import tpu as pltpu
from jax.sharding import PartitionSpec as P

MESH = pl.DeviceIdType.MESH
PANEL = 256
NPANEL = 4
HALO = 32
ROWS = 512
WIN = 512
Q = 128
R = 64
NX = 4
NZ = 4
NCHAN = 16
NBAND = 16
PLANES = 4
CHANNELS = ROWS * NCHAN
BINS = 32
WB = WIN // NBAND
F32 = jnp.float32
BF16 = jnp.bfloat16

PLAN = (
    ("raw", 0), ("power", 0), ("prepare", 0), ("raw", 1), ("pick", 0), ("pick", 1), ("merge", 0), ("merge", 1),
    ("sum_y", 0), ("share_z", 0), ("pick", 2), ("share_z", 1), ("pick", 3), ("band_sum", 0), ("raw", 2),
    ("pass_z", 0), ("merge", 2), ("pass_z", 1), ("merge", 3), ("raw", 3), ("window", 0), ("share_x", 0),
    ("share_z", 2), ("pick", 4), ("share_z", 3), ("share_x", 1), ("pick", 5), ("own_y", 0), ("pass_z", 2),
    ("merge", 4), ("pick", 6), ("pass_z", 3), ("choose", 0), ("own_core", 0), ("merge", 5), ("share_x", 2),
    ("pick", 7), ("pass_x", 0), ("share_z", 4), ("merge", 6), ("own_norm", 1), ("share_x", 3), ("pass_x", 1),
    ("gathered", 0), ("own_norm", 0), ("share_z", 5), ("merge", 7), ("pass_x", 2), ("pass_z", 4), ("share_z", 6),
    ("panel_y", 0), ("pass_x", 3), ("pass_z", 5), ("share_z", 7), ("share_x", 4), ("pass_z", 6), ("share_x", 5),
    ("pass_z", 7), ("panel_core", 0), ("share_x", 6), ("pass_x", 4), ("share_x", 7), ("panel_scale", 0),
    ("multiply", 0), ("pass_x", 6), ("pass_x", 5), ("multiply", 1), ("pass_x", 7), ("multiply", 2), ("multiply", 3),
)


def root(fourth):
    return lax.rsqrt(jnp.sqrt(jnp.sqrt(fourth)))


def move_kernel(
    spec_hbm, width_hbm, block_hbm, offset_hbm, out_hbm, left_hbm, right_hbm,
    spec, width, block, offset, a0, a1, a2, a3, b0, b1, b2, b3, b4, b5, b6, b7,
    m0, m1, m2, m3, m4, m5, m6, m7, gath, picked, onehot, power, bands, near, total,
    cand, parts, means, scale, left, out, right, l_s, o_s, a_s, a_r, rz_s, rz_r, gz_s, gz_r, gx_s, gx_r, e_s, e_r, rb_s, rb_r, rc_s, rc_r, gc_s, gc_r, gb_s, gb_r,
):
    c, b = lax.axis_index("chan"), lax.axis_index("band")
    x, z = c // NZ, c % NZ
    core = b % 2
    half_band = b // 2

    def windows_of(t):
        return t % 2 * 8 + t // 2 % 4 * 2 + t // 8

    wb = windows_of(b)
    a, zb = (a0, a1, a2, a3), (b0, b1, b2, b3, b4, b5, b6, b7)
    mo = (m0, m1, m2, m3, m4, m5, m6, m7)

    def at_x(d):
        return ((x + d) % NX * NZ + z, b)

    def at_z(d):
        return (x * NZ + (z + d) % NZ, b)

    def at_c(d):
        return ((c + d) % NCHAN, b)

    def at_b(d):
        return (c, (b + d) % NBAND)

    def block_of(i, size, count=None):
        return pl.ds(pl.multiple_of(i * size, size), count or size)

    def send(src, dst, ssem, rsem, dev):
        copy = pltpu.make_async_remote_copy(
            src_ref=src, dst_ref=dst, send_sem=ssem, recv_sem=rsem, device_id=dev, device_id_type=MESH
        )
        copy.start()
        return copy

    loads = [
        pltpu.make_async_copy(src, dst, l_s.at[i])
        for i, (src, dst) in enumerate(
            ((spec_hbm, spec), (width_hbm, width), (block_hbm, block), (offset_hbm, offset))
        )
    ]
    for cp in loads:
        cp.start()
    barrier = pltpu.get_barrier_semaphore()
    for d in range(1, NCHAN):
        pl.semaphore_signal(barrier, inc=1, device_id=at_c(d), device_id_type=MESH)
    for d in range(1, NBAND):
        pl.semaphore_signal(barrier, inc=1, device_id=at_b(d), device_id_type=MESH)
    pl.semaphore_wait(barrier, NCHAN + NBAND - 2)

    a_cp = [None] * PLANES

    def raw(q):
        a_cp[q] = []
        for d in (1, 3, 2):
            src = spec_hbm.at[q // 2, q % 2, :, block_of((x + d) % NX, Q)]
            a_cp[q].append(send(src, a[q].at[d], a_s.at[q, d], a_r.at[q, d], at_x(d)))

    def own_power(_):
        for cp in loads:
            cp.wait()
        for i in range(ROWS // Q):
            acc = jnp.zeros((Q, WIN), F32)
            for f in range(2):
                for k in range(2):
                    v = spec[f, k, i * Q : (i + 1) * Q, :].astype(F32)
                    acc = acc + v * v
            for j in range(WIN // Q):
                power[j * Q : (j + 1) * Q, i * Q : (i + 1) * Q] = acc[:, j * Q : (j + 1) * Q].T.astype(BF16)
        st["rb"] = []
        for d in range(1, 8):
            t = b // 8 * 8 + (b + d) % 8
            src = power.at[block_of(windows_of(t) // 2, 2 * WB), :]
            st["rb"].append(send(src, bands.at[d], rb_s.at[d], rb_r.at[d], (c, t)))

    def prepare(_):
        for q in range(PLANES):
            a[q][0] = spec[q // 2, q % 2, :, block_of(x, Q)]
        for p in range(NPANEL):
            here = lax.broadcasted_iota(jnp.int32, (PANEL, ROWS), 1)
            want = lax.broadcasted_iota(jnp.int32, (PANEL, ROWS), 0) + offset[p]
            onehot[p] = jnp.where(here == want, 1.0, 0.0).astype(BF16)

    st = {}

    def wait(name):
        for cp in st[name]:
            cp.wait_recv()

    arrived = set()

    def pick(u):
        q, h = u // 2, u % 2
        if q not in arrived:
            arrived.add(q)
            for cp in a_cp[q]:
                cp.wait_recv()
        for p in (2 * h, 2 * h + 1):
            slot = lax.rem(x - block[p] // NZ + NX, NX)
            picked[q, p] = jnp.dot(onehot[p], a[q][slot], preferred_element_type=F32).astype(BF16)
        zb[u][0] = picked[q, 2 * h : 2 * h + 2, block_of(z, R), :]
        rows = block_of((z + 2) % NZ, R)
        st["ro", u] = [
            send(picked.at[q, 2 * h + i, rows, :], mo[u].at[i, 1], rz_s.at[u, 2 * i], rz_r.at[u, 2 * i], at_z(d))
            for i, d in enumerate((3, 1))
        ]
        for i, d in enumerate((3, 1)):
            mo[u][i, 0] = picked[q, 2 * h + i, block_of((z + d) % NZ, R), :]

    def merge(u):
        q, h = u // 2, u % 2
        wait(("ro", u))
        st["rz", u] = []
        for i, d in enumerate((3, 1)):
            rows = block_of((z + d) % NZ, R)
            theirs = jnp.where(block[2 * h + i] % NZ == (z + NZ - d) % NZ, 1, 0)
            picked[q, 2 * h + i, rows, :] = mo[u][i, theirs]
            src = picked.at[q, pl.ds(2 * h, 2), rows, :]
            s = 3 - 2 * i
            st["rz", u].append(send(src, zb[u].at[2 - i], rz_s.at[u, s], rz_r.at[u, s], at_z(d)))

    def share_z(u):
        q, h = u // 2, u % 2
        wait(("rz", u))
        for i in range(2):
            away = lax.rem(z - block[2 * h + i] % NZ + NZ, NZ)
            slot = jnp.minimum(away, 2) if i == 0 else away - away // 2
            gath[q // 2, 2 * h + i, q % 2, block_of(z, R), block_of(x, Q)] = zb[u][slot, i]
        part = gath.at[q // 2, pl.ds(2 * h, 2), q % 2, block_of(z, R), block_of(x, Q)]
        st["gz", u] = [send(part, part, gz_s.at[u, i], gz_r.at[u, i], at_z(d)) for i, d in enumerate((1, 3))]

    def pass_z(u):
        q, h = u // 2, u % 2
        st["fz", u] = []
        for i, (came, to) in enumerate(((3, 1), (1, 3))):
            st["gz", u][i].wait_recv()
            part = gath.at[q // 2, 2 * h + i, q % 2, block_of((z + came) % NZ, R), block_of(x, Q)]
            st["fz", u].append(send(part, part, gz_s.at[u, 2 + i], gz_r.at[u, 2 + i], at_z(to)))

    def share_x(u):
        q, h = u // 2, u % 2
        wait(("fz", u))
        part = gath.at[q // 2, pl.ds(2 * h, 2), q % 2, :, block_of(x, Q)]
        st["gx", u] = [send(part, part, gx_s.at[u, i], gx_r.at[u, i], at_x(d)) for i, d in enumerate((1, 3))]

    def pass_x(u):
        q, h = u // 2, u % 2
        st["fx", u] = []
        for i, (came, to) in enumerate(((3, 1), (1, 3))):
            st["gx", u][i].wait_recv()
            part = gath.at[q // 2, 2 * h + i, q % 2, :, block_of((x + came) % NX, Q)]
            st["fx", u].append(send(part, part, gx_s.at[u, 2 + i], gx_r.at[u, 2 + i], at_x(to)))

    mine = block_of(wb, WB)
    pair = block_of(wb // 2, 2 * WB)
    own_lanes, panel_lanes = pl.ds(0, ROWS), pl.ds(ROWS, NPANEL * PANEL)

    def near_sum(_):
        wait("rb")
        acc = power[pair, :].astype(F32)
        for d in range(1, 8):
            acc = acc + bands[d].astype(F32)
        near[0] = acc
        other = near.at[0, block_of((wb + 1) % 2, WB), :]
        st["rs"] = [send(other, near.at[1, pl.ds(0, WB), :], rb_s.at[8], rb_r.at[8], at_b(8))]

    def band_sum(_):
        wait("rs")
        total[:, Q : Q + ROWS] = near[0, block_of(wb % 2, WB), :] + near[1, 0:WB, :]
        st["e"] = [
            send(total.at[:, pl.ds(ROWS, Q)], total.at[:, pl.ds(0, Q)], e_s.at[0], e_r.at[0], at_c(1)),
            send(total.at[:, pl.ds(Q, Q)], total.at[:, pl.ds(ROWS + Q, Q)], e_s.at[1], e_r.at[1], at_c(15)),
        ]

    def window(_):
        wait("e")
        wide = ROWS + 2 * Q
        chan = lax.broadcasted_iota(jnp.int32, (WB, wide), 1) + (c * ROWS - Q)
        ext = jnp.where((chan >= 0) & (chan < CHANNELS), total[...], 0.0)
        row = lax.broadcasted_iota(jnp.int32, (WB, ROWS), 0)
        half = jnp.zeros((WB, ROWS), jnp.int32)
        for i in range(WB):
            half = jnp.where(row == i, width[wb * WB + i], half)
        win = ext[:, Q : Q + ROWS]
        for o in range(1, HALO + 1):
            both = pltpu.roll(ext, o, 1) + pltpu.roll(ext, wide - o, 1)
            win = win + jnp.where(half >= o, both[:, Q : Q + ROWS], 0.0)
        chan = lax.broadcasted_iota(jnp.int32, (WB, ROWS), 1) + c * ROWS
        count = jnp.minimum(chan + half, CHANNELS - 1) - jnp.maximum(chan - half, 0) + 1
        mean = win / (count.astype(F32) * BINS) + 1e-6
        mean = ((mean * mean) * (mean * mean)).astype(BF16)
        means[mine, own_lanes] = mean
        part = means.at[mine, own_lanes]
        st["oz"] = [send(part, part, gb_s.at[0], gb_r.at[0], at_b(8))]
        for p in range(NPANEL):
            cand[:, p * PANEL : (p + 1) * PANEL] = lax.dot_general(
                mean, onehot[p], (((1,), (1,)), ((), ())), preferred_element_type=F32
            ).astype(BF16)
        st["rc"] = []
        for d in range(1, NCHAN):
            t = (c + d) % NCHAN
            src = cand.at[block_of(t % 2, 16), block_of(t // 2, Q)]
            st["rc"].append(send(src, parts.at[d], rc_s.at[d], rc_r.at[d], at_c(d)))
        parts[0] = cand[block_of(c % 2, 16), block_of(c // 2, Q)]

    def choose(_):
        wait("rc")
        mine_too = means.at[pl.ds(pl.multiple_of(wb * WB + c % 2 * 16, 16), 16), pl.ds(pl.multiple_of(ROWS + c // 2 * Q, Q), Q)]
        mine_too[...] = parts[lax.rem(c - block[c // 4] + NCHAN, NCHAN)]
        st["gc"] = [send(mine_too, mine_too, gc_s.at[d], gc_r.at[d], at_c(d)) for d in range(1, NCHAN)]

    def gathered(_):
        wait("gc")
        part = means.at[mine, panel_lanes]
        st["pz"] = [send(part, part, gb_s.at[8], gb_r.at[8], at_b(8))]

    def along_y(here, there, lanes, sem):
        wait(here)
        st[there] = []
        for d in range(1, 4):
            t = (c, b // 8 * 8 + (b % 8 + 2 * d) % 8)
            part = means.at[pair, lanes]
            st[there].append(send(part, part, gb_s.at[sem + d], gb_r.at[sem + d], t))

    def to_core(here, there, lanes, sem):
        wait(here)
        part = means.at[block_of(core, WIN // 2), lanes]
        st[there] = [send(part, part, gb_s.at[sem], gb_r.at[sem], (c, half_band * 2 + (core + 1) % 2))]

    stores, owned = [], []

    def own_norm(half):
        if not owned:
            wait("ok")
        owned.append(half)
        for i in range(2 * half, 2 * half + 2):
            for j in range(WIN // Q):
                s = root(means[j * Q : (j + 1) * Q, i * Q : (i + 1) * Q].astype(F32)).T
                for f in range(2):
                    for k in range(2):
                        v = spec[f, k, i * Q : (i + 1) * Q, j * Q : (j + 1) * Q].astype(F32)
                        left[f, i * Q : (i + 1) * Q, k * WIN + j * Q : k * WIN + (j + 1) * Q] = (v * s).astype(BF16)
        rows = pl.ds(half * 2 * Q, 2 * Q)
        stores.append(pltpu.make_async_copy(left.at[1, rows], left_hbm.at[rows], o_s.at[4 + half]))
        stores[-1].start()

    def panel_scale(_):
        wait("pk")
        for p in range(NPANEL):
            for i in range(PANEL // Q):
                lanes = slice(ROWS + p * PANEL + i * Q, ROWS + p * PANEL + (i + 1) * Q)
                for j in range(WIN // Q):
                    scale[p, i * Q : (i + 1) * Q, j * Q : (j + 1) * Q] = root(
                        means[j * Q : (j + 1) * Q, lanes].astype(F32)
                    ).T

    def multiply(v):
        f, h = v // 2, v % 2
        wait(("fx", 4 * f + h))
        wait(("fx", 4 * f + 2 + h))

        def body(p, carry):
            re = (gath[f, p, 0].astype(F32) * scale[p]).astype(BF16)
            im = (gath[f, p, 1].astype(F32) * scale[p]).astype(BF16)
            for k, right in enumerate((jnp.concatenate([re, im], axis=1), jnp.concatenate([-im, re], axis=1))):
                gram = lax.dot_general(left[f], right, (((1,), (1,)), ((), ())), preferred_element_type=F32)
                out[p, f, k] = (gram * WIN ** (-0.5)).astype(BF16)
            return carry

        if v < 3:
            lax.fori_loop(2 * h, 2 * h + 2, body, 0)
        else:
            for i in range(2):
                for k in range(2):
                    right[i, :, k * WIN : (k + 1) * WIN] = (gath[1, 2 + i, k].astype(F32) * scale[2 + i]).astype(BF16)
            src, dst = right, right_hbm
        if v < 3:
            src, dst = out.at[pl.ds(2 * h, 2), f], out_hbm.at[v]
        stores.append(pltpu.make_async_copy(src, dst, o_s.at[v]))
        stores[-1].start()

    steps = {
        "raw": raw, "power": own_power, "prepare": prepare,
        "pick": pick, "merge": merge, "share_z": share_z, "pass_z": pass_z, "share_x": share_x, "pass_x": pass_x, "multiply": multiply,
        "sum_y": near_sum, "band_sum": band_sum, "window": window, "choose": choose, "gathered": gathered,
        "own_y": lambda _: along_y("oz", "oy", own_lanes, 0),
        "own_core": lambda _: to_core("oy", "ok", own_lanes, 7),
        "panel_y": lambda _: along_y("pz", "py", panel_lanes, 8),
        "panel_core": lambda _: to_core("py", "pk", panel_lanes, 15),
        "own_norm": own_norm, "panel_scale": panel_scale,
    }
    for name, q in PLAN:
        steps[name](q)
    for group in a_cp + list(st.values()):
        for cp in group:
            cp.wait_send()
    for cp in stores:
        cp.wait()


def finish_kernel(products, left_hbm, right_hbm, out, held, left, right, fresh, in_sem, out_sem):
    first = [
        pltpu.make_async_copy(left_hbm, left, in_sem.at[0]),
        pltpu.make_async_copy(right_hbm.at[0], right.at[0], in_sem.at[1]),
        pltpu.make_async_copy(right_hbm.at[1], right.at[1], in_sem.at[2]),
    ]
    pieces = [(v, i) for v in range(3) for i in range(2)]
    get = [pltpu.make_async_copy(products.at[v, i], held.at[v, i], in_sem.at[3 + n]) for n, (v, i) in enumerate(pieces)]
    put = [
        pltpu.make_async_copy(held.at[v, i], out.at[2 * (v % 2) + i, v // 2], out_sem.at[n])
        for n, (v, i) in enumerate(pieces)
    ]
    late = [pltpu.make_async_copy(fresh.at[i], out.at[2 + i, 1], out_sem.at[6 + i]) for i in range(2)]
    for cp in first + get:
        cp.start()
    first[0].wait()
    for i in range(2):
        first[1 + i].wait()
        re, im = right[i, :, :WIN], right[i, :, WIN:]
        for k, factor in enumerate((right[i], jnp.concatenate([-im, re], axis=1))):
            gram = lax.dot_general(left[...], factor, (((1,), (1,)), ((), ())), preferred_element_type=F32)
            fresh[i, k] = (gram * WIN ** (-0.5)).astype(BF16)
        late[i].start()
        for n in range(3 * i, 3 * i + 3):
            get[n].wait()
            put[n].start()
    for cp in put + late:
        cp.wait()


def local(spectra, half_width, panel_block, panel_offset):
    dma = pltpu.SemaphoreType.DMA
    hbm = pl.BlockSpec(memory_space=pltpu.HBM)
    products, left, right = pl.pallas_call(
        move_kernel,
        out_shape=(
            jax.ShapeDtypeStruct((3, 2, 2, ROWS, PANEL), BF16),
            jax.ShapeDtypeStruct((ROWS, 2 * WIN), BF16),
            jax.ShapeDtypeStruct((2, PANEL, 2 * WIN), BF16),
        ),
        in_specs=[hbm] * 4,
        out_specs=(hbm, hbm, hbm),
        scratch_shapes=[
            pltpu.VMEM((2, 2, ROWS, WIN), BF16),
            pltpu.SMEM((WIN,), jnp.int32),
            pltpu.SMEM((NPANEL,), jnp.int32),
            pltpu.SMEM((NPANEL,), jnp.int32),
        ]
        + [pltpu.VMEM((NX, ROWS, Q), BF16)] * 4
        + [pltpu.VMEM((3, 2, R, Q), BF16)] * 8
        + [pltpu.VMEM((2, 2, R, Q), BF16)] * 8
        + [
            pltpu.VMEM((2, NPANEL, 2, PANEL, WIN), BF16),
            pltpu.VMEM((PLANES, NPANEL, PANEL, Q), BF16),
            pltpu.VMEM((NPANEL, PANEL, ROWS), BF16),
            pltpu.VMEM((WIN, ROWS), BF16),
            pltpu.VMEM((8, 2 * WB, ROWS), BF16),
            pltpu.VMEM((2, 2 * WB, ROWS), F32),
            pltpu.VMEM((WB, ROWS + 2 * Q), F32),
            pltpu.VMEM((WB, NPANEL * PANEL), BF16),
            pltpu.VMEM((NCHAN, 16, Q), BF16),
            pltpu.VMEM((WIN, ROWS + NPANEL * PANEL), BF16),
            pltpu.VMEM((NPANEL, PANEL, WIN), F32),
            pltpu.VMEM((2, ROWS, 2 * WIN), BF16),
            pltpu.VMEM((NPANEL, 2, 2, ROWS, PANEL), BF16),
            pltpu.VMEM((2, PANEL, 2 * WIN), BF16),
            dma((4,)),
            dma((6,)),
        ]
        + [dma((4, 4))] * 2
        + [dma((8, 4))] * 6
        + [dma((2,))] * 2
        + [dma((16,))] * 8,
        compiler_params=pltpu.CompilerParams(
            collective_id=0, has_side_effects=True, vmem_limit_bytes=60 * 1024 * 1024
        ),
        name="cross_spectra",
    )(spectra, half_width, panel_block, panel_offset)
    return pl.pallas_call(
        finish_kernel,
        out_shape=jax.ShapeDtypeStruct((NPANEL, 2, 2, ROWS, PANEL), BF16),
        in_specs=[hbm] * 3,
        out_specs=hbm,
        scratch_shapes=[
            pltpu.VMEM((3, 2, 2, ROWS, PANEL), BF16),
            pltpu.VMEM((ROWS, 2 * WIN), BF16),
            pltpu.VMEM((2, PANEL, 2 * WIN), BF16),
            pltpu.VMEM((2, 2, ROWS, PANEL), BF16),
            dma((9,)),
            dma((8,)),
        ],
        compiler_params=pltpu.CompilerParams(vmem_limit_bytes=60 * 1024 * 1024),
        name="finish",
    )(products, left, right)


def solution(mesh):
    placed = (P("band", None, "chan", None), P(), P(), P())
    return jax.shard_map(
        local,
        mesh=mesh,
        in_specs=placed,
        out_specs=P(None, "band", None, "chan", None),
        check_vma=False,
    )
```

```python
import jax
import jax.numpy as jnp
from jax import lax
from jax.experimental import pallas as pl
from jax.experimental.pallas import tpu as pltpu
from jax.sharding import PartitionSpec as P

MESH = pl.DeviceIdType.MESH
PANEL = 256
NPANEL = 4
HALO = 32
ROWS = 512
WIN = 512
Q = 128
R = 64
NX = 4
NZ = 4
NCHAN = 16
NBAND = 16
PLANES = 4
CHANNELS = ROWS * NCHAN
BINS = 32
WB = WIN // NBAND
F32 = jnp.float32
BF16 = jnp.bfloat16

PLAN = (
    ("raw", 0), ("power", 0), ("prepare", 0), ("raw", 1), ("pick", 0), ("pick", 1), ("merge", 0), ("merge", 1),
    ("sum_y", 0), ("share_z", 0), ("pick", 3), ("pick", 2), ("share_z", 1), ("band_sum", 0), ("raw", 3),
    ("pass_z", 0), ("merge", 3), ("merge", 2), ("raw", 2), ("pass_z", 1), ("window", 0), ("share_x", 0),
    ("share_z", 3), ("pick", 6), ("share_x", 1), ("share_z", 2), ("pick", 7), ("own_y", 0), ("pass_z", 3),
    ("merge", 6), ("pick", 4), ("choose", 0), ("own_core", 0), ("pass_z", 2), ("merge", 7), ("share_x", 3),
    ("pick", 5), ("share_z", 6), ("pass_x", 0), ("merge", 4), ("own_norm", 1), ("pass_x", 1), ("share_x", 2),
    ("gathered", 0), ("own_norm", 0), ("share_z", 7), ("merge", 5), ("pass_x", 3), ("pass_z", 6), ("share_z", 4),
    ("panel_y", 0), ("pass_z", 7), ("pass_x", 2), ("share_z", 5), ("share_x", 6), ("pass_z", 4), ("share_x", 7),
    ("pass_z", 5), ("panel_core", 0), ("share_x", 4), ("pass_x", 6), ("share_x", 5), ("panel_scale", 0),
    ("multiply", 1), ("pass_x", 4), ("pass_x", 7), ("multiply", 0), ("pass_x", 5), ("multiply", 2), ("multiply", 3),
)


def root(fourth):
    return lax.rsqrt(jnp.sqrt(jnp.sqrt(fourth)))


def move_kernel(
    spec_hbm, width_hbm, block_hbm, offset_hbm, out_hbm, left_hbm, right_hbm,
    spec, width, block, offset, a0, a1, a2, a3, b0, b1, b2, b3, b4, b5, b6, b7,
    m0, m1, m2, m3, m4, m5, m6, m7, gath, picked, onehot, power, bands, near, total,
    cand, parts, means, scale, left, out, right, l_s, o_s, a_s, a_r, rz_s, rz_r, gz_s, gz_r, gx_s, gx_r, e_s, e_r, rb_s, rb_r, rc_s, rc_r, gc_s, gc_r, gb_s, gb_r,
):
    c, b = lax.axis_index("chan"), lax.axis_index("band")
    x, z = c // NZ, c % NZ
    core = b % 2
    half_band = b // 2

    def windows_of(t):
        return t % 2 * 8 + t // 2 % 4 * 2 + t // 8

    wb = windows_of(b)
    a, zb = (a0, a1, a2, a3), (b0, b1, b2, b3, b4, b5, b6, b7)
    mo = (m0, m1, m2, m3, m4, m5, m6, m7)

    def at_x(d):
        return ((x + d) % NX * NZ + z, b)

    def at_z(d):
        return (x * NZ + (z + d) % NZ, b)

    def at_c(d):
        return ((c + d) % NCHAN, b)

    def at_b(d):
        return (c, (b + d) % NBAND)

    def block_of(i, size, count=None):
        return pl.ds(pl.multiple_of(i * size, size), count or size)

    def send(src, dst, ssem, rsem, dev):
        copy = pltpu.make_async_remote_copy(
            src_ref=src, dst_ref=dst, send_sem=ssem, recv_sem=rsem, device_id=dev, device_id_type=MESH
        )
        copy.start()
        return copy

    loads = [
        pltpu.make_async_copy(src, dst, l_s.at[i])
        for i, (src, dst) in enumerate(
            ((spec_hbm, spec), (width_hbm, width), (block_hbm, block), (offset_hbm, offset))
        )
    ]
    for cp in loads:
        cp.start()
    barrier = pltpu.get_barrier_semaphore()
    for d in range(1, NCHAN):
        pl.semaphore_signal(barrier, inc=1, device_id=at_c(d), device_id_type=MESH)
    for d in range(1, NBAND):
        pl.semaphore_signal(barrier, inc=1, device_id=at_b(d), device_id_type=MESH)
    pl.semaphore_wait(barrier, NCHAN + NBAND - 2)

    a_cp = [None] * PLANES

    def raw(q):
        a_cp[q] = []
        for d in (1, 3, 2):
            src = spec_hbm.at[q // 2, q % 2, :, block_of((x + d) % NX, Q)]
            a_cp[q].append(send(src, a[q].at[d], a_s.at[q, d], a_r.at[q, d], at_x(d)))

    def own_power(_):
        for cp in loads:
            cp.wait()
        for i in range(ROWS // Q):
            acc = jnp.zeros((Q, WIN), F32)
            for f in range(2):
                for k in range(2):
                    v = spec[f, k, i * Q : (i + 1) * Q, :].astype(F32)
                    acc = acc + v * v
            for j in range(WIN // Q):
                power[j * Q : (j + 1) * Q, i * Q : (i + 1) * Q] = acc[:, j * Q : (j + 1) * Q].T.astype(BF16)
        st["rb"] = []
        for d in range(1, 8):
            t = b // 8 * 8 + (b + d) % 8
            src = power.at[block_of(windows_of(t) // 2, 2 * WB), :]
            st["rb"].append(send(src, bands.at[d], rb_s.at[d], rb_r.at[d], (c, t)))

    def prepare(_):
        for q in range(PLANES):
            a[q][0] = spec[q // 2, q % 2, :, block_of(x, Q)]
        for p in range(NPANEL):
            here = lax.broadcasted_iota(jnp.int32, (PANEL, ROWS), 1)
            want = lax.broadcasted_iota(jnp.int32, (PANEL, ROWS), 0) + offset[p]
            onehot[p] = jnp.where(here == want, 1.0, 0.0).astype(BF16)

    st = {}

    def wait(name):
        for cp in st[name]:
            cp.wait_recv()

    arrived = set()

    def pick(u):
        q, h = u // 2, u % 2
        if q not in arrived:
            arrived.add(q)
            for cp in a_cp[q]:
                cp.wait_recv()
        for p in (2 * h, 2 * h + 1):
            slot = lax.rem(x - block[p] // NZ + NX, NX)
            picked[q, p] = jnp.dot(onehot[p], a[q][slot], preferred_element_type=F32).astype(BF16)
        zb[u][0] = picked[q, 2 * h : 2 * h + 2, block_of(z, R), :]
        rows = block_of((z + 2) % NZ, R)
        st["ro", u] = [
            send(picked.at[q, 2 * h + i, rows, :], mo[u].at[i, 1], rz_s.at[u, 2 * i], rz_r.at[u, 2 * i], at_z(d))
            for i, d in enumerate((3, 1))
        ]
        for i, d in enumerate((3, 1)):
            mo[u][i, 0] = picked[q, 2 * h + i, block_of((z + d) % NZ, R), :]

    def merge(u):
        q, h = u // 2, u % 2
        wait(("ro", u))
        st["rz", u] = []
        for i, d in enumerate((3, 1)):
            rows = block_of((z + d) % NZ, R)
            theirs = jnp.where(block[2 * h + i] % NZ == (z + NZ - d) % NZ, 1, 0)
            picked[q, 2 * h + i, rows, :] = mo[u][i, theirs]
            src = picked.at[q, pl.ds(2 * h, 2), rows, :]
            s = 3 - 2 * i
            st["rz", u].append(send(src, zb[u].at[2 - i], rz_s.at[u, s], rz_r.at[u, s], at_z(d)))

    def share_z(u):
        q, h = u // 2, u % 2
        wait(("rz", u))
        for i in range(2):
            away = lax.rem(z - block[2 * h + i] % NZ + NZ, NZ)
            slot = jnp.minimum(away, 2) if i == 0 else away - away // 2
            gath[q // 2, 2 * h + i, q % 2, block_of(z, R), block_of(x, Q)] = zb[u][slot, i]
        part = gath.at[q // 2, pl.ds(2 * h, 2), q % 2, block_of(z, R), block_of(x, Q)]
        st["gz", u] = [send(part, part, gz_s.at[u, i], gz_r.at[u, i], at_z(d)) for i, d in enumerate((1, 3))]

    def pass_z(u):
        q, h = u // 2, u % 2
        st["fz", u] = []
        for i, (came, to) in enumerate(((3, 1), (1, 3))):
            st["gz", u][i].wait_recv()
            part = gath.at[q // 2, 2 * h + i, q % 2, block_of((z + came) % NZ, R), block_of(x, Q)]
            st["fz", u].append(send(part, part, gz_s.at[u, 2 + i], gz_r.at[u, 2 + i], at_z(to)))

    def share_x(u):
        q, h = u // 2, u % 2
        wait(("fz", u))
        part = gath.at[q // 2, pl.ds(2 * h, 2), q % 2, :, block_of(x, Q)]
        st["gx", u] = [send(part, part, gx_s.at[u, i], gx_r.at[u, i], at_x(d)) for i, d in enumerate((1, 3))]

    def pass_x(u):
        q, h = u // 2, u % 2
        st["fx", u] = []
        for i, (came, to) in enumerate(((3, 1), (1, 3))):
            st["gx", u][i].wait_recv()
            part = gath.at[q // 2, 2 * h + i, q % 2, :, block_of((x + came) % NX, Q)]
            st["fx", u].append(send(part, part, gx_s.at[u, 2 + i], gx_r.at[u, 2 + i], at_x(to)))

    mine = block_of(wb, WB)
    pair = block_of(wb // 2, 2 * WB)
    own_lanes, panel_lanes = pl.ds(0, ROWS), pl.ds(ROWS, NPANEL * PANEL)

    def near_sum(_):
        wait("rb")
        acc = power[pair, :].astype(F32)
        for d in range(1, 8):
            acc = acc + bands[d].astype(F32)
        near[0] = acc
        other = near.at[0, block_of((wb + 1) % 2, WB), :]
        st["rs"] = [send(other, near.at[1, pl.ds(0, WB), :], rb_s.at[8], rb_r.at[8], at_b(8))]

    def band_sum(_):
        wait("rs")
        total[:, Q : Q + ROWS] = near[0, block_of(wb % 2, WB), :] + near[1, 0:WB, :]
        st["e"] = [
            send(total.at[:, pl.ds(ROWS, Q)], total.at[:, pl.ds(0, Q)], e_s.at[0], e_r.at[0], at_c(1)),
            send(total.at[:, pl.ds(Q, Q)], total.at[:, pl.ds(ROWS + Q, Q)], e_s.at[1], e_r.at[1], at_c(15)),
        ]

    def window(_):
        wait("e")
        wide = ROWS + 2 * Q
        chan = lax.broadcasted_iota(jnp.int32, (WB, wide), 1) + (c * ROWS - Q)
        ext = jnp.where((chan >= 0) & (chan < CHANNELS), total[...], 0.0)
        row = lax.broadcasted_iota(jnp.int32, (WB, ROWS), 0)
        half = jnp.zeros((WB, ROWS), jnp.int32)
        for i in range(WB):
            half = jnp.where(row == i, width[wb * WB + i], half)
        win = ext[:, Q : Q + ROWS]
        for o in range(1, HALO + 1):
            both = pltpu.roll(ext, o, 1) + pltpu.roll(ext, wide - o, 1)
            win = win + jnp.where(half >= o, both[:, Q : Q + ROWS], 0.0)
        chan = lax.broadcasted_iota(jnp.int32, (WB, ROWS), 1) + c * ROWS
        count = jnp.minimum(chan + half, CHANNELS - 1) - jnp.maximum(chan - half, 0) + 1
        mean = win / (count.astype(F32) * BINS) + 1e-6
        mean = ((mean * mean) * (mean * mean)).astype(BF16)
        means[mine, own_lanes] = mean
        part = means.at[mine, own_lanes]
        st["oz"] = [send(part, part, gb_s.at[0], gb_r.at[0], at_b(8))]
        for p in range(NPANEL):
            cand[:, p * PANEL : (p + 1) * PANEL] = lax.dot_general(
                mean, onehot[p], (((1,), (1,)), ((), ())), preferred_element_type=F32
            ).astype(BF16)
        st["rc"] = []
        for d in range(1, NCHAN):
            t = (c + d) % NCHAN
            src = cand.at[block_of(t % 2, 16), block_of(t // 2, Q)]
            st["rc"].append(send(src, parts.at[d], rc_s.at[d], rc_r.at[d], at_c(d)))
        parts[0] = cand[block_of(c % 2, 16), block_of(c // 2, Q)]

    def choose(_):
        wait("rc")
        mine_too = means.at[pl.ds(pl.multiple_of(wb * WB + c % 2 * 16, 16), 16), pl.ds(pl.multiple_of(ROWS + c // 2 * Q, Q), Q)]
        mine_too[...] = parts[lax.rem(c - block[c // 4] + NCHAN, NCHAN)]
        st["gc"] = [send(mine_too, mine_too, gc_s.at[d], gc_r.at[d], at_c(d)) for d in range(1, NCHAN)]

    def gathered(_):
        wait("gc")
        part = means.at[mine, panel_lanes]
        st["pz"] = [send(part, part, gb_s.at[8], gb_r.at[8], at_b(8))]

    def along_y(here, there, lanes, sem):
        wait(here)
        st[there] = []
        for d in range(1, 4):
            t = (c, b // 8 * 8 + (b % 8 + 2 * d) % 8)
            part = means.at[pair, lanes]
            st[there].append(send(part, part, gb_s.at[sem + d], gb_r.at[sem + d], t))

    def to_core(here, there, lanes, sem):
        wait(here)
        part = means.at[block_of(core, WIN // 2), lanes]
        st[there] = [send(part, part, gb_s.at[sem], gb_r.at[sem], (c, half_band * 2 + (core + 1) % 2))]

    stores, owned = [], []

    def own_norm(half):
        if not owned:
            wait("ok")
        owned.append(half)
        for i in range(2 * half, 2 * half + 2):
            for j in range(WIN // Q):
                s = root(means[j * Q : (j + 1) * Q, i * Q : (i + 1) * Q].astype(F32)).T
                for f in range(2):
                    for k in range(2):
                        v = spec[f, k, i * Q : (i + 1) * Q, j * Q : (j + 1) * Q].astype(F32)
                        left[f, i * Q : (i + 1) * Q, k * WIN + j * Q : k * WIN + (j + 1) * Q] = (v * s).astype(BF16)
        rows = pl.ds(half * 2 * Q, 2 * Q)
        stores.append(pltpu.make_async_copy(left.at[1, rows], left_hbm.at[rows], o_s.at[4 + half]))
        stores[-1].start()

    def panel_scale(_):
        wait("pk")
        for p in range(NPANEL):
            for i in range(PANEL // Q):
                lanes = slice(ROWS + p * PANEL + i * Q, ROWS + p * PANEL + (i + 1) * Q)
                for j in range(WIN // Q):
                    scale[p, i * Q : (i + 1) * Q, j * Q : (j + 1) * Q] = root(
                        means[j * Q : (j + 1) * Q, lanes].astype(F32)
                    ).T

    def multiply(v):
        f, h = v // 2, v % 2
        wait(("fx", 4 * f + h))
        wait(("fx", 4 * f + 2 + h))

        def body(p, carry):
            re = (gath[f, p, 0].astype(F32) * scale[p]).astype(BF16)
            im = (gath[f, p, 1].astype(F32) * scale[p]).astype(BF16)
            for k, right in enumerate((jnp.concatenate([re, im], axis=1), jnp.concatenate([-im, re], axis=1))):
                gram = lax.dot_general(left[f], right, (((1,), (1,)), ((), ())), preferred_element_type=F32)
                out[p, f, k] = (gram * WIN ** (-0.5)).astype(BF16)
            return carry

        if v < 3:
            lax.fori_loop(2 * h, 2 * h + 2, body, 0)
        else:
            for i in range(2):
                for k in range(2):
                    right[i, :, k * WIN : (k + 1) * WIN] = (gath[1, 2 + i, k].astype(F32) * scale[2 + i]).astype(BF16)
            src, dst = right, right_hbm
        if v < 3:
            src, dst = out.at[pl.ds(2 * h, 2), f], out_hbm.at[v]
        stores.append(pltpu.make_async_copy(src, dst, o_s.at[v]))
        stores[-1].start()

    steps = {
        "raw": raw, "power": own_power, "prepare": prepare,
        "pick": pick, "merge": merge, "share_z": share_z, "pass_z": pass_z, "share_x": share_x, "pass_x": pass_x, "multiply": multiply,
        "sum_y": near_sum, "band_sum": band_sum, "window": window, "choose": choose, "gathered": gathered,
        "own_y": lambda _: along_y("oz", "oy", own_lanes, 0),
        "own_core": lambda _: to_core("oy", "ok", own_lanes, 7),
        "panel_y": lambda _: along_y("pz", "py", panel_lanes, 8),
        "panel_core": lambda _: to_core("py", "pk", panel_lanes, 15),
        "own_norm": own_norm, "panel_scale": panel_scale,
    }
    for name, q in PLAN:
        steps[name](q)
    for group in a_cp + list(st.values()):
        for cp in group:
            cp.wait_send()
    for cp in stores:
        cp.wait()


def finish_kernel(products, left_hbm, right_hbm, out, held, left, right, fresh, in_sem, out_sem):
    first = [
        pltpu.make_async_copy(left_hbm, left, in_sem.at[0]),
        pltpu.make_async_copy(right_hbm.at[0], right.at[0], in_sem.at[1]),
        pltpu.make_async_copy(right_hbm.at[1], right.at[1], in_sem.at[2]),
    ]
    pieces = [(v, i) for v in range(3) for i in range(2)]
    get = [pltpu.make_async_copy(products.at[v, i], held.at[v, i], in_sem.at[3 + n]) for n, (v, i) in enumerate(pieces)]
    put = [
        pltpu.make_async_copy(held.at[v, i], out.at[2 * (v % 2) + i, v // 2], out_sem.at[n])
        for n, (v, i) in enumerate(pieces)
    ]
    late = [pltpu.make_async_copy(fresh.at[i], out.at[2 + i, 1], out_sem.at[6 + i]) for i in range(2)]
    for cp in first + get:
        cp.start()
    first[0].wait()
    for i in range(2):
        first[1 + i].wait()
        re, im = right[i, :, :WIN], right[i, :, WIN:]
        for k, factor in enumerate((right[i], jnp.concatenate([-im, re], axis=1))):
            gram = lax.dot_general(left[...], factor, (((1,), (1,)), ((), ())), preferred_element_type=F32)
            fresh[i, k] = (gram * WIN ** (-0.5)).astype(BF16)
        late[i].start()
        for n in range(3 * i, 3 * i + 3):
            get[n].wait()
            put[n].start()
    for cp in put + late:
        cp.wait()


def local(spectra, half_width, panel_block, panel_offset):
    dma = pltpu.SemaphoreType.DMA
    hbm = pl.BlockSpec(memory_space=pltpu.HBM)
    products, left, right = pl.pallas_call(
        move_kernel,
        out_shape=(
            jax.ShapeDtypeStruct((3, 2, 2, ROWS, PANEL), BF16),
            jax.ShapeDtypeStruct((ROWS, 2 * WIN), BF16),
            jax.ShapeDtypeStruct((2, PANEL, 2 * WIN), BF16),
        ),
        in_specs=[hbm] * 4,
        out_specs=(hbm, hbm, hbm),
        scratch_shapes=[
            pltpu.VMEM((2, 2, ROWS, WIN), BF16),
            pltpu.SMEM((WIN,), jnp.int32),
            pltpu.SMEM((NPANEL,), jnp.int32),
            pltpu.SMEM((NPANEL,), jnp.int32),
        ]
        + [pltpu.VMEM((NX, ROWS, Q), BF16)] * 4
        + [pltpu.VMEM((3, 2, R, Q), BF16)] * 8
        + [pltpu.VMEM((2, 2, R, Q), BF16)] * 8
        + [
            pltpu.VMEM((2, NPANEL, 2, PANEL, WIN), BF16),
            pltpu.VMEM((PLANES, NPANEL, PANEL, Q), BF16),
            pltpu.VMEM((NPANEL, PANEL, ROWS), BF16),
            pltpu.VMEM((WIN, ROWS), BF16),
            pltpu.VMEM((8, 2 * WB, ROWS), BF16),
            pltpu.VMEM((2, 2 * WB, ROWS), F32),
            pltpu.VMEM((WB, ROWS + 2 * Q), F32),
            pltpu.VMEM((WB, NPANEL * PANEL), BF16),
            pltpu.VMEM((NCHAN, 16, Q), BF16),
            pltpu.VMEM((WIN, ROWS + NPANEL * PANEL), BF16),
            pltpu.VMEM((NPANEL, PANEL, WIN), F32),
            pltpu.VMEM((2, ROWS, 2 * WIN), BF16),
            pltpu.VMEM((NPANEL, 2, 2, ROWS, PANEL), BF16),
            pltpu.VMEM((2, PANEL, 2 * WIN), BF16),
            dma((4,)),
            dma((6,)),
        ]
        + [dma((4, 4))] * 2
        + [dma((8, 4))] * 6
        + [dma((2,))] * 2
        + [dma((16,))] * 8,
        compiler_params=pltpu.CompilerParams(
            collective_id=0, has_side_effects=True, vmem_limit_bytes=60 * 1024 * 1024
        ),
        name="cross_spectra",
    )(spectra, half_width, panel_block, panel_offset)
    return pl.pallas_call(
        finish_kernel,
        out_shape=jax.ShapeDtypeStruct((NPANEL, 2, 2, ROWS, PANEL), BF16),
        in_specs=[hbm] * 3,
        out_specs=hbm,
        scratch_shapes=[
            pltpu.VMEM((3, 2, 2, ROWS, PANEL), BF16),
            pltpu.VMEM((ROWS, 2 * WIN), BF16),
            pltpu.VMEM((2, PANEL, 2 * WIN), BF16),
            pltpu.VMEM((2, 2, ROWS, PANEL), BF16),
            dma((9,)),
            dma((8,)),
        ],
        compiler_params=pltpu.CompilerParams(vmem_limit_bytes=60 * 1024 * 1024),
        name="finish",
    )(products, left, right)


def solution(mesh):
    placed = (P("band", None, "chan", None), P(), P(), P())
    return jax.shard_map(
        local,
        mesh=mesh,
        in_specs=placed,
        out_specs=P(None, "band", None, "chan", None),
        check_vma=False,
    )
```
